32 devices in a mesh: section: 8 (over z, x), band: 4 (over y, core).
Axes of the slice: x: 2, y: 2, z: 4, core: 2. Of those that a mesh axis runs over, the one named last changes fastest.
Arguments:
- echoes: bfloat16 [2, 4096, 2, 16384], P(None, ('band', 'section')), may hold values from -6 to 6
- replica: float32 [2, 2048], replicated, may hold values from -0.09375 to 0.09375
- azimuth_taps: float32 [256, 2, 1024], P(('section', 'band')), may hold values from -0.125 to 0.125
- coefficients: bfloat16 [256, 8, 64, 128], P(('section', 'band')), may hold values from -2 to 2
- offsets: int32 [256, 128], P(('section', 'band')), may hold values from 0 to 57
- block_order: int32 [2], replicated, may hold values from 0 to 1, each once
Outputs:
- image: bfloat16 [2, 16384, 2, 4096], P(None, ('section', 'band'))
The draws below stay inside these ranges and needn't reach their ends.
Inputs may be any that keep to these rules, and one draw needn't show every extreme that they name: `block_order`: each block appears once.
All inputs are finite; a program needn't handle non-finite values.
Results may differ from the reference program's by a relative error of at most 0.015.
Values may be sent and summed in bfloat16 or wider, within the bound.
A program may use at most 256 MiB of HBM per device.

```python
import math
import jax
import jax.numpy as jnp
from jax import lax

RANGE_BINS = 16384
PULSES = 4096
FACTOR = 128
CHIRP_TAPS = 2048
AZIMUTH_TAPS = 1024
BAND_BINS = 64
MARGIN_BINS = 32
KERNEL = 8
BLOCKS = 2
MIGRATION_BANDS = 256


def draw_offsets(key, part):
    highest = 2 * MARGIN_BINS - KERNEL + 1
    values = jax.random.randint(key, (MIGRATION_BANDS, FACTOR), 0, highest + 1, dtype=jnp.int32)
    values = values.at[0, 0].set(0)
    return values.at[MIGRATION_BANDS - 1, FACTOR - 1].set(highest)


def block_levels(rng, dims, shards, least, high):
    loudness, own = 1.0, jax.random.fold_in(rng, 6)
    for position, blocks in shards:
        draws = jnp.exp(jax.random.uniform(jax.random.fold_in(own, position), (blocks,), jnp.float32, least / len(shards), high / len(shards)))
        loudness = loudness * jnp.repeat(draws, dims[position] // blocks).reshape([-1 if axis == position else 1 for axis in range(len(dims))])
    return loudness


def scatter_about(rng, shape, width, most, pieces=(), kind=jnp.bfloat16):
    factor_of = block_levels(rng, shape, pieces, -0.22, 0.18) if pieces else 1.0
    result = jax.random.normal(rng, shape, jnp.float32) * width * factor_of
    return jnp.minimum(jnp.maximum(result, -most), most).astype(kind)


def setup_inputs(seed: int = 0) -> dict:
    key_of = jax.random.split(jax.random.key(seed), 7)
    echoes = scatter_about(key_of[0], (BLOCKS, PULSES, 2, RANGE_BINS), 1.0, 6.0, ((1, 32),))
    replica = scatter_about(key_of[1], (2, CHIRP_TAPS), (2 * CHIRP_TAPS) ** -0.5, 0.09375, (), jnp.float32)
    azimuth_taps = scatter_about(key_of[2], (MIGRATION_BANDS, 2, AZIMUTH_TAPS), (2 * AZIMUTH_TAPS) ** -0.5, 0.125, ((0, 32),), jnp.float32)
    coefficients = scatter_about(key_of[3], (MIGRATION_BANDS, KERNEL, BAND_BINS, FACTOR), KERNEL ** -0.5, 2.0, ((0, 32),))
    offsets = draw_offsets(jax.random.fold_in(key_of[6], 71), 0)
    block_order = jax.random.permutation(key_of[5], BLOCKS).astype(jnp.int32)
    return {"echoes": echoes, "replica": replica, "azimuth_taps": azimuth_taps, "coefficients": coefficients, "offsets": offsets, "block_order": block_order}


def phases(outer_size, inner_size, length):
    outer_index = jnp.arange(outer_size, dtype=jnp.int32)[:, None]
    inner_index = jnp.arange(inner_size, dtype=jnp.int32)[None, :]
    return (2.0 * math.pi / length) * ((outer_index * inner_index) % length).astype(jnp.float32)


def left_matrix(phase_table, signum):
    cosine = jnp.cos(phase_table)
    sine_part = signum * jnp.sin(phase_table)
    upper_rows = jnp.stack([cosine, -sine_part], axis=1)
    lower_rows = jnp.stack([sine_part, cosine], axis=1)
    return jnp.stack([upper_rows, lower_rows], axis=0)


def right_matrix(phase_table, signum):
    cosine = jnp.cos(phase_table)
    sine_part = signum * jnp.sin(phase_table)
    leading = jnp.stack([cosine, sine_part], axis=1)
    trailing = jnp.stack([-sine_part, cosine], axis=1)
    return jnp.stack([leading, trailing], axis=0)


def rotate_by(real_part, imag_part, phase_table, signum):
    cosine = jnp.cos(phase_table)
    sine_part = signum * jnp.sin(phase_table)
    return real_part * cosine - imag_part * sine_part, real_part * sine_part + imag_part * cosine


def make_tables(length):
    outer_size = length // FACTOR
    outer_phase = phases(outer_size, outer_size, outer_size)
    inner_phase = phases(FACTOR, FACTOR, FACTOR)
    twist_phase = phases(outer_size, FACTOR, length)
    return (left_matrix(outer_phase, -1.0).astype(jnp.bfloat16), right_matrix(inner_phase, -1.0).astype(jnp.bfloat16), twist_phase, left_matrix(outer_phase, 1.0).astype(jnp.bfloat16), right_matrix(inner_phase, 1.0).astype(jnp.bfloat16))


def contract(pattern, left_side, right_side):
    left_side = lax.optimization_barrier(left_side).astype(jnp.float32)
    right_side = lax.optimization_barrier(right_side).astype(jnp.float32)
    return jnp.einsum(pattern, left_side, right_side)


def exact_spectrum(tap_rows, length):
    outer_size = length // FACTOR
    padded = jnp.pad(tap_rows, ((0, 0), (0, 0), (0, length - tap_rows.shape[2])))
    padded = padded.reshape(tap_rows.shape[0], 2, outer_size, FACTOR)
    outer_phase = phases(outer_size, outer_size, outer_size)
    inner_phase = phases(FACTOR, FACTOR, FACTOR)
    twist_phase = phases(outer_size, FACTOR, length)
    mixed_rows = jnp.einsum('ckdn,bdnm->bckm', left_matrix(outer_phase, -1.0), padded, precision=lax.Precision.HIGHEST)
    real_part, imag_part = rotate_by(mixed_rows[:, 0], mixed_rows[:, 1], twist_phase, -1.0)
    rotated = jnp.stack([real_part, imag_part], axis=1)
    return jnp.einsum('bdkn,dnem->bkem', rotated, right_matrix(inner_phase, -1.0), precision=lax.Precision.HIGHEST)


def first_pass(signal, tables):
    mixed_rows = contract('ckdn,bdnm->bckm', tables[0], signal)
    real_part, imag_part = rotate_by(mixed_rows[:, 0], mixed_rows[:, 1], tables[2], -1.0)
    rotated = jnp.stack([real_part, imag_part], axis=1).astype(jnp.bfloat16)
    return contract('bdkn,dnem->bkem', rotated, tables[1])


def matched(values, spectrum):
    real_part = values[..., 0, :]
    imag_part = values[..., 1, :]
    spec_real = spectrum[..., 0, :]
    spec_imag = spectrum[..., 1, :]
    return jnp.stack([real_part * spec_real + imag_part * spec_imag, imag_part * spec_real - real_part * spec_imag], axis=-2).astype(jnp.bfloat16)


def finish(filtered, tables, length, pattern):
    returned = contract('bkdn,dnem->bkem', filtered, tables[4])
    real_part, imag_part = rotate_by(returned[:, :, 0], returned[:, :, 1], tables[2], 1.0)
    turned = jnp.stack([real_part, imag_part], axis=1).astype(jnp.bfloat16)
    return (contract(pattern, tables[3], turned) * (1.0 / length)).astype(jnp.bfloat16)


def compress_range(signal, spectrum, tables):
    pulse_rows = signal.shape[0]
    outer_size = RANGE_BINS // FACTOR
    spectral = first_pass(signal.reshape(pulse_rows, 2, outer_size, FACTOR), tables)
    filtered = matched(spectral, spectrum)
    return finish(filtered, tables, RANGE_BINS, 'cmek,bekq->mqcb').reshape(RANGE_BINS, 2, pulse_rows)


def build_migration(coefficients, offsets):
    columns = jnp.arange(BAND_BINS + 2 * MARGIN_BINS, dtype=jnp.int32)[None, None, :, None]
    targets = jnp.arange(BAND_BINS, dtype=jnp.int32)[None, :, None, None] + offsets[:, None, None, :]
    migration_table = jnp.zeros((coefficients.shape[0], BAND_BINS, BAND_BINS + 2 * MARGIN_BINS, coefficients.shape[3]), jnp.float32)
    for tap_index in range(KERNEL):
        weights = coefficients[:, tap_index, :, None, :].astype(jnp.float32)
        migration_table = migration_table + jnp.where(columns == targets + tap_index, weights, jnp.zeros((), jnp.float32))
    return migration_table.astype(jnp.bfloat16)


def focus_block(compressed, spectra, coefficients, offsets, tables):
    outer_size = PULSES // FACTOR
    spectral = first_pass(compressed.reshape(RANGE_BINS, 2, outer_size, FACTOR), tables).astype(jnp.bfloat16)
    padded = jnp.pad(spectral, ((MARGIN_BINS, MARGIN_BINS), (0, 0), (0, 0), (0, 0)))

    def one_band(band_index):
        window = lax.dynamic_slice_in_dim(padded, (band_index * BAND_BINS).astype(jnp.int32), BAND_BINS + 2 * MARGIN_BINS, 0)
        migration_table = build_migration(coefficients[band_index][None], offsets[band_index][None])
        shifted = contract('jitg,jtkcg->jikcg', migration_table, window[None])
        filtered = matched(shifted, spectra[band_index][None, None])
        return finish(filtered.reshape(BAND_BINS, outer_size, 2, FACTOR), tables, PULSES, 'cmek,bekq->bcmq')

    focused = lax.map(one_band, jnp.arange(MIGRATION_BANDS, dtype=jnp.int32))
    return focused.reshape(RANGE_BINS, 2, PULSES)


def reference(echoes, replica, azimuth_taps, coefficients, offsets, block_order):
    range_tables = make_tables(RANGE_BINS)
    pulse_tables = make_tables(PULSES)
    range_spectrum = exact_spectrum(replica[None], RANGE_BINS)[0]
    spectra = exact_spectrum(azimuth_taps, PULSES)

    def one_block(block_index):
        signal = lax.dynamic_index_in_dim(echoes, block_index, 0, keepdims=False)
        compressed = compress_range(signal, range_spectrum, range_tables)
        return focus_block(compressed, spectra, coefficients, offsets, pulse_tables)

    return lax.map(one_block, block_order)
```

```python
import functools
import math

import jax
import jax.numpy as jnp
from jax import lax
from jax.experimental import pallas as pl
from jax.experimental.pallas import tpu as pltpu
from jax.sharding import PartitionSpec as P

RANGE_BINS = 16384
PULSES = 4096
FACTOR = 128
BAND_BINS = 64
MARGIN_BINS = 32
KERNEL = 8
BLOCKS = 2


def extended(cells, sides, width):
    for axis, dim in sides:
        count = lax.axis_size(axis)
        ends = count - 1
        head = lax.slice_in_dim(cells, 0, width, axis=dim)
        tail = lax.slice_in_dim(cells, cells.shape[dim] - width, cells.shape[dim], axis=dim)
        cells = jnp.concatenate(
            [
                lax.ppermute(tail, axis, [(i, (i + 1) % count) for i in range(ends)]),
                cells,
                lax.ppermute(head, axis, [((i + 1) % count, i) for i in range(ends)]),
            ],
            axis=dim,
        )
    return cells


def phases(outer_size, inner_size, length):
    outer_index = jnp.arange(outer_size, dtype=jnp.int32)[:, None]
    inner_index = jnp.arange(inner_size, dtype=jnp.int32)[None, :]
    return 2.0 * math.pi / length * (outer_index * inner_index % length).astype(jnp.float32)


def left_matrix(phase_table, signum):
    cosine = jnp.cos(phase_table)
    sine_part = signum * jnp.sin(phase_table)
    upper_rows = jnp.stack([cosine, -sine_part], axis=1)
    lower_rows = jnp.stack([sine_part, cosine], axis=1)
    return jnp.stack([upper_rows, lower_rows], axis=0)


def right_matrix(phase_table, signum):
    cosine = jnp.cos(phase_table)
    sine_part = signum * jnp.sin(phase_table)
    leading = jnp.stack([cosine, sine_part], axis=1)
    trailing = jnp.stack([-sine_part, cosine], axis=1)
    return jnp.stack([leading, trailing], axis=0)


def rotate_by(real_part, imag_part, phase_table, signum):
    cosine = jnp.cos(phase_table)
    sine_part = signum * jnp.sin(phase_table)
    return (real_part * cosine - imag_part * sine_part, real_part * sine_part + imag_part * cosine)


def make_tables(length):
    outer_size = length // FACTOR
    outer_phase = phases(outer_size, outer_size, outer_size)
    inner_phase = phases(FACTOR, FACTOR, FACTOR)
    twist_phase = phases(outer_size, FACTOR, length)
    return (
        left_matrix(outer_phase, -1.0).astype(jnp.bfloat16),
        right_matrix(inner_phase, -1.0).astype(jnp.bfloat16),
        twist_phase,
        left_matrix(outer_phase, 1.0).astype(jnp.bfloat16),
        right_matrix(inner_phase, 1.0).astype(jnp.bfloat16),
    )


def contract(pattern, left_side, right_side):
    return jnp.einsum(pattern, left_side, right_side, preferred_element_type=jnp.float32)


def exact_spectrum(tap_rows, length):
    outer_size = length // FACTOR
    padded = jnp.pad(tap_rows, ((0, 0), (0, 0), (0, length - tap_rows.shape[2])))
    padded = padded.reshape(tap_rows.shape[0], 2, outer_size, FACTOR)
    outer_phase = phases(outer_size, outer_size, outer_size)
    inner_phase = phases(FACTOR, FACTOR, FACTOR)
    twist_phase = phases(outer_size, FACTOR, length)
    mixed_rows = jnp.einsum(
        "ckdn,bdnm->bckm", left_matrix(outer_phase, -1.0), padded, precision=lax.Precision.HIGHEST
    )
    real_part, imag_part = rotate_by(mixed_rows[:, 0], mixed_rows[:, 1], twist_phase, -1.0)
    rotated = jnp.stack([real_part, imag_part], axis=1)
    return jnp.einsum(
        "bdkn,dnem->bkem", rotated, right_matrix(inner_phase, -1.0), precision=lax.Precision.HIGHEST
    )


def matched(values, spectrum):
    real_part = values[..., 0, :]
    imag_part = values[..., 1, :]
    spec_real = spectrum[..., 0, :]
    spec_imag = spectrum[..., 1, :]
    return jnp.stack(
        [
            real_part * spec_real + imag_part * spec_imag,
            imag_part * spec_real - real_part * spec_imag,
        ],
        axis=-2,
    ).astype(jnp.bfloat16)


def compress_range(signal, spectrum, tables):
    pulse_rows = signal.shape[0]
    outer_size = RANGE_BINS // FACTOR
    mixed_rows = contract(
        "ckdn,bdnm->bckm", tables[0], signal.reshape(pulse_rows, 2, outer_size, FACTOR)
    )
    real_part, imag_part = rotate_by(mixed_rows[:, 0], mixed_rows[:, 1], tables[2], -1.0)
    rotated = jnp.stack([real_part, imag_part], axis=1).astype(jnp.bfloat16)
    spectral = contract("bdkn,dnem->bkem", rotated, tables[1])
    filtered = matched(spectral, spectrum)
    returned = contract("bkdn,dnem->bkem", filtered, tables[4])
    real_part, imag_part = rotate_by(returned[:, :, 0], returned[:, :, 1], tables[2], 1.0)
    turned = jnp.stack([real_part, imag_part], axis=1).astype(jnp.bfloat16)
    lines = (contract("cmek,bekq->bcmq", tables[3], turned) * (1.0 / RANGE_BINS)).astype(
        jnp.bfloat16
    )
    return lines.reshape(pulse_rows, 2, RANGE_BINS)


def build_migration(coefficients, offsets):
    columns = jnp.arange(BAND_BINS + 2 * MARGIN_BINS, dtype=jnp.int32)[None, None, :, None]
    targets = (
        jnp.arange(BAND_BINS, dtype=jnp.int32)[None, :, None, None] + offsets[:, None, None, :]
    )
    migration_table = jnp.zeros(
        (coefficients.shape[0], BAND_BINS, BAND_BINS + 2 * MARGIN_BINS, coefficients.shape[3]),
        jnp.float32,
    )
    for tap_index in range(KERNEL):
        weights = coefficients[:, tap_index, :, None, :].astype(jnp.float32)
        migration_table = migration_table + jnp.where(
            columns == targets + tap_index, weights, jnp.zeros((), jnp.float32)
        )
    return migration_table.astype(jnp.bfloat16)


def migrate(padded, migration_table):
    range_rows = padded.shape[3] - 2 * MARGIN_BINS
    band_count = range_rows // BAND_BINS
    lead = padded.shape[:3]
    head_rows = padded[..., :range_rows].reshape(lead + (band_count, BAND_BINS))
    tail_rows = padded[..., BAND_BINS : BAND_BINS + range_rows].reshape(
        lead + (band_count, BAND_BINS)
    )
    window = jnp.concatenate([head_rows, tail_rows], axis=4)
    shifted = contract("jitg,kcgjt->kcgji", migration_table, window)
    return shifted.reshape(lead + (range_rows,))


def focus_azimuth(turned, migration_table, band_spectra, tables):
    range_rows = turned.shape[2]
    outer_size = PULSES // FACTOR
    signal = turned.reshape(outer_size, FACTOR, 2, range_rows)
    mixed_rows = contract("ckdn,nmdr->kmcr", tables[0], signal)
    twist = tables[2][:, :, None]
    real_part, imag_part = rotate_by(mixed_rows[:, :, 0], mixed_rows[:, :, 1], twist, -1.0)
    rotated = jnp.stack([real_part, imag_part], axis=2).astype(jnp.bfloat16)
    spectral = contract("kndr,dnem->kemr", rotated, tables[1]).astype(jnp.bfloat16)
    padded = extended(spectral, ((("section", "band"), 3),), MARGIN_BINS)
    moved = migrate(padded, migration_table)
    real_part = moved[:, 0]
    imag_part = moved[:, 1]
    spec_real = band_spectra[:, 0]
    spec_imag = band_spectra[:, 1]
    filtered = jnp.stack(
        [
            real_part * spec_real + imag_part * spec_imag,
            imag_part * spec_real - real_part * spec_imag,
        ],
        axis=1,
    ).astype(jnp.bfloat16)
    returned = contract("kdnr,dnem->kemr", filtered, tables[4])
    real_part, imag_part = rotate_by(returned[:, 0], returned[:, 1], twist, 1.0)
    back = jnp.stack([real_part, imag_part], axis=1).astype(jnp.bfloat16)
    focused = (contract("cmek,keqr->rcmq", tables[3], back) * (1.0 / PULSES)).astype(jnp.bfloat16)
    return focused.reshape(range_rows, 2, PULSES)


def corner_turn(compressed):
    pulse_rows = compressed.shape[0]
    block_count = compressed.shape[1]
    sections = lax.axis_size("section")
    band_count = lax.axis_size("band")
    local_rows = RANGE_BINS // (sections * band_count)
    shaped = compressed.reshape(1, 1, pulse_rows, block_count, 2, sections, band_count, local_rows)
    across_bands = lax.all_to_all(shaped, "band", split_axis=6, concat_axis=0, tiled=True)
    across_sections = lax.all_to_all(
        across_bands, "section", split_axis=5, concat_axis=1, tiled=True
    )
    arrived = across_sections.reshape(
        band_count * sections * pulse_rows, block_count, 2, local_rows
    )
    return arrived


def compress_send_kernel(
    axes,
    x_ref,
    left_ref,
    right_ref,
    right_back_ref,
    left_back_ref,
    cosine_ref,
    sine_ref,
    spec_real_ref,
    spec_imag_ref,
    arrived_ref,
    outbox,
    send_sem,
    recv_sem,
    local_sem,
):
    (major, major_size), (minor, minor_size) = axes
    count = major_size * minor_size
    step = pl.program_id(0)
    steps = pl.num_programs(0)
    pairs = outbox.shape[2]
    per_block = arrived_ref.shape[2] // pairs
    block = step // per_block
    first = (step % per_block) * pairs
    me = lax.axis_index(major) * minor_size + lax.axis_index(minor)
    source = lax.axis_index(minor) * major_size + lax.axis_index(major)

    @pl.when(step == 0)
    def _():
        barrier = pltpu.get_barrier_semaphore()

        def greet(k, carry):
            other = (me + k) % count
            pl.semaphore_signal(
                barrier,
                inc=1,
                device_id={major: other // minor_size, minor: other % minor_size},
                device_id_type=pl.DeviceIdType.MESH,
            )
            return carry

        lax.fori_loop(1, count, greet, 0)
        pl.semaphore_wait(barrier, count - 1)

    left = left_ref[...]
    right = right_ref[...]
    right_back = right_back_ref[...]
    left_back = left_back_ref[...]
    half = FACTOR

    def one_pair(pair, carry):
        cosine = cosine_ref[...]
        sine = sine_ref[...]
        spec_real = spec_real_ref[...]
        spec_imag = spec_imag_ref[...]
        signal = jnp.concatenate([x_ref[0, 2 * pair], x_ref[0, 2 * pair + 1]], axis=1)
        mixed = jnp.dot(left, signal, preferred_element_type=jnp.float32)
        rows = []
        for p in range(2):
            lanes = slice(p * half, (p + 1) * half)
            re, im = mixed[:half, lanes], mixed[half:, lanes]
            rows.append(
                jnp.concatenate([re * cosine + im * sine, im * cosine - re * sine], axis=1).astype(
                    jnp.bfloat16
                )
            )
        spectral = jnp.dot(
            jnp.concatenate(rows, axis=0), right, preferred_element_type=jnp.float32
        )
        rows = []
        for p in range(2):
            part = spectral[p * half : (p + 1) * half]
            re, im = part[:, :half], part[:, half:]
            rows.append(
                jnp.concatenate(
                    [re * spec_real + im * spec_imag, im * spec_real - re * spec_imag], axis=1
                ).astype(jnp.bfloat16)
            )
        returned = jnp.dot(
            jnp.concatenate(rows, axis=0), right_back, preferred_element_type=jnp.float32
        )
        columns = []
        for p in range(2):
            part = returned[p * half : (p + 1) * half]
            re, im = part[:, :half], part[:, half:]
            columns.append(
                jnp.concatenate([re * cosine - im * sine, re * sine + im * cosine], axis=0).astype(
                    jnp.bfloat16
                )
            )
        lines = jnp.dot(
            left_back, jnp.concatenate(columns, axis=1), preferred_element_type=jnp.float32
        ) * (1.0 / RANGE_BINS)
        tile = lines.shape[0] // count
        packed = jnp.concatenate(
            [
                lines[:, :half].reshape(count, tile, half),
                lines[:, half:].reshape(count, tile, half),
            ],
            axis=1,
        ).astype(jnp.bfloat16)
        outbox[step, :, pair] = packed
        return carry

    lax.fori_loop(0, pairs, one_pair, 0)

    own = pltpu.make_async_copy(
        outbox.at[step, me], arrived_ref.at[block, source, pl.ds(first, pairs)], local_sem
    )
    own.start()

    def post(k, carry):
        other = (me + k * 11) % count
        pltpu.make_async_remote_copy(
            src_ref=outbox.at[step, other],
            dst_ref=arrived_ref.at[block, source, pl.ds(first, pairs)],
            send_sem=send_sem,
            recv_sem=recv_sem,
            device_id={major: other // minor_size, minor: other % minor_size},
            device_id_type=pl.DeviceIdType.MESH,
        ).start()
        return carry

    lax.fori_loop(1, count, post, 0)
    own.wait()

    @pl.when(step == steps - 1)
    def _():
        whole = arrived_ref.at[:, pl.ds(0, count - 1)]
        pltpu.make_async_copy(whole, whole, send_sem).wait()
        pltpu.make_async_copy(whole, whole, recv_sem).wait()


def compress_and_turn(echoes, spectrum, axes):
    blocks, pulses, _, length = echoes.shape
    count = axes[0][1] * axes[1][1]
    outer_size = length // FACTOR
    rows_each = outer_size // count
    chunk = 16
    signal = (
        echoes.reshape(blocks, pulses, 2, outer_size, FACTOR)
        .transpose(0, 1, 3, 2, 4)
        .reshape(blocks, pulses, 2 * outer_size, FACTOR)
    )
    tables = make_tables(length)
    left = tables[0].transpose(0, 1, 3, 2).reshape(2 * outer_size, 2 * outer_size)
    right = tables[1].reshape(2 * FACTOR, 2 * FACTOR)
    right_back = tables[4].reshape(2 * FACTOR, 2 * FACTOR)
    left_back = (
        tables[3]
        .reshape(2, count, rows_each, 2 * outer_size)
        .transpose(1, 0, 2, 3)
        .reshape(2 * outer_size, 2 * outer_size)
    )
    steps_per_block = pulses // chunk
    steps = blocks * steps_per_block
    pairs = chunk // 2
    tile = 4 * rows_each

    def whole(array):
        return pl.BlockSpec(array.shape, lambda s: (0,) * array.ndim)

    operands = (
        left,
        right,
        right_back,
        left_back,
        jnp.cos(tables[2]),
        jnp.sin(tables[2]),
        spectrum[:, 0],
        spectrum[:, 1],
    )
    return pl.pallas_call(
        functools.partial(compress_send_kernel, axes),
        grid=(steps,),
        in_specs=[
            pl.BlockSpec(
                (1, chunk, 2 * outer_size, FACTOR),
                lambda s: (s // steps_per_block, s % steps_per_block, 0, 0),
            )
        ]
        + [whole(array) for array in operands],
        out_specs=pl.BlockSpec(memory_space=pl.ANY),
        out_shape=jax.ShapeDtypeStruct(
            (blocks, count, pulses // 2, tile, FACTOR), jnp.bfloat16
        ),
        scratch_shapes=[
            pltpu.VMEM((steps, count, pairs, tile, FACTOR), jnp.bfloat16),
            pltpu.SemaphoreType.DMA,
            pltpu.SemaphoreType.DMA,
            pltpu.SemaphoreType.DMA,
        ],
        compiler_params=pltpu.CompilerParams(
            collective_id=0, has_side_effects=True, vmem_limit_bytes=44 * 2**20
        ),
        cost_estimate=pl.CostEstimate(
            flops=blocks * pulses * 16 * FACTOR**2 * 2 * FACTOR,
            bytes_accessed=4 * echoes.size,
            transcendentals=0,
        ),
        name="compress_turn",
    )(signal, *operands)


def on_device(echoes, replica, azimuth_taps, coefficients, offsets, block_order):
    sections = lax.axis_size("section")
    bands = lax.axis_size("band")
    count = sections * bands
    direct = (RANGE_BINS // FACTOR) == 4 * count and echoes.shape[1] % 16 == 0
    range_tables = make_tables(RANGE_BINS)
    pulse_tables = make_tables(PULSES)
    range_spectrum = exact_spectrum(replica[None], RANGE_BINS)[0]
    spectra = exact_spectrum(azimuth_taps, PULSES)
    band_spectra = jnp.repeat(jnp.transpose(spectra, (1, 2, 3, 0)), BAND_BINS, axis=3)
    migration_table = build_migration(coefficients, offsets)
    if direct:
        arrived = compress_and_turn(
            echoes, range_spectrum, (("section", sections), ("band", bands))
        ).reshape(echoes.shape[0], PULSES, 2, RANGE_BINS // count)
    images = []
    for position in range(BLOCKS):
        if direct:
            turned = lax.dynamic_index_in_dim(arrived, block_order[position], 0, keepdims=False)
        else:
            signal = lax.dynamic_index_in_dim(echoes, block_order[position], 0, keepdims=False)
            compressed = compress_range(signal, range_spectrum, range_tables)
            turned = corner_turn(compressed[:, None])[:, 0]
        images.append(focus_azimuth(turned, migration_table, band_spectra, pulse_tables))
    return jnp.stack(images, axis=0)


def solution(mesh):
    in_specs = (
        P(None, ("band", "section"), None, None),
        P(),
        P(("section", "band"), None, None),
        P(("section", "band"), None, None, None),
        P(("section", "band"), None),
        P(),
    )
    out_specs = P(None, ("section", "band"), None, None)
    return jax.shard_map(
        on_device, mesh=mesh, in_specs=in_specs, out_specs=out_specs, check_vma=False
    )
```

```python
import functools
import math

import jax
import jax.numpy as jnp
from jax import lax
from jax.experimental import pallas as pl
from jax.experimental.pallas import tpu as pltpu
from jax.sharding import PartitionSpec as P

RANGE_BINS = 16384
PULSES = 4096
FACTOR = 128
BAND_BINS = 64
MARGIN_BINS = 32
KERNEL = 8
BLOCKS = 2


def extended(cells, sides, width):
    for axis, dim in sides:
        count = lax.axis_size(axis)
        ends = count - 1
        head = lax.slice_in_dim(cells, 0, width, axis=dim)
        tail = lax.slice_in_dim(cells, cells.shape[dim] - width, cells.shape[dim], axis=dim)
        cells = jnp.concatenate(
            [
                lax.ppermute(tail, axis, [(i, (i + 1) % count) for i in range(ends)]),
                cells,
                lax.ppermute(head, axis, [((i + 1) % count, i) for i in range(ends)]),
            ],
            axis=dim,
        )
    return cells


def phases(outer_size, inner_size, length):
    outer_index = jnp.arange(outer_size, dtype=jnp.int32)[:, None]
    inner_index = jnp.arange(inner_size, dtype=jnp.int32)[None, :]
    return 2.0 * math.pi / length * (outer_index * inner_index % length).astype(jnp.float32)


def left_matrix(phase_table, signum):
    cosine = jnp.cos(phase_table)
    sine_part = signum * jnp.sin(phase_table)
    upper_rows = jnp.stack([cosine, -sine_part], axis=1)
    lower_rows = jnp.stack([sine_part, cosine], axis=1)
    return jnp.stack([upper_rows, lower_rows], axis=0)


def right_matrix(phase_table, signum):
    cosine = jnp.cos(phase_table)
    sine_part = signum * jnp.sin(phase_table)
    leading = jnp.stack([cosine, sine_part], axis=1)
    trailing = jnp.stack([-sine_part, cosine], axis=1)
    return jnp.stack([leading, trailing], axis=0)


def rotate_by(real_part, imag_part, phase_table, signum):
    cosine = jnp.cos(phase_table)
    sine_part = signum * jnp.sin(phase_table)
    return (real_part * cosine - imag_part * sine_part, real_part * sine_part + imag_part * cosine)


def make_tables(length):
    outer_size = length // FACTOR
    outer_phase = phases(outer_size, outer_size, outer_size)
    inner_phase = phases(FACTOR, FACTOR, FACTOR)
    twist_phase = phases(outer_size, FACTOR, length)
    return (
        left_matrix(outer_phase, -1.0).astype(jnp.bfloat16),
        right_matrix(inner_phase, -1.0).astype(jnp.bfloat16),
        twist_phase,
        left_matrix(outer_phase, 1.0).astype(jnp.bfloat16),
        right_matrix(inner_phase, 1.0).astype(jnp.bfloat16),
    )


def contract(pattern, left_side, right_side):
    return jnp.einsum(pattern, left_side, right_side, preferred_element_type=jnp.float32)


def exact_spectrum(tap_rows, length):
    outer_size = length // FACTOR
    padded = jnp.pad(tap_rows, ((0, 0), (0, 0), (0, length - tap_rows.shape[2])))
    padded = padded.reshape(tap_rows.shape[0], 2, outer_size, FACTOR)
    outer_phase = phases(outer_size, outer_size, outer_size)
    inner_phase = phases(FACTOR, FACTOR, FACTOR)
    twist_phase = phases(outer_size, FACTOR, length)
    mixed_rows = jnp.einsum(
        "ckdn,bdnm->bckm", left_matrix(outer_phase, -1.0), padded, precision=lax.Precision.HIGHEST
    )
    real_part, imag_part = rotate_by(mixed_rows[:, 0], mixed_rows[:, 1], twist_phase, -1.0)
    rotated = jnp.stack([real_part, imag_part], axis=1)
    return jnp.einsum(
        "bdkn,dnem->bkem", rotated, right_matrix(inner_phase, -1.0), precision=lax.Precision.HIGHEST
    )


def matched(values, spectrum):
    real_part = values[..., 0, :]
    imag_part = values[..., 1, :]
    spec_real = spectrum[..., 0, :]
    spec_imag = spectrum[..., 1, :]
    return jnp.stack(
        [
            real_part * spec_real + imag_part * spec_imag,
            imag_part * spec_real - real_part * spec_imag,
        ],
        axis=-2,
    ).astype(jnp.bfloat16)


def compress_range(signal, spectrum, tables):
    pulse_rows = signal.shape[0]
    outer_size = RANGE_BINS // FACTOR
    mixed_rows = contract(
        "ckdn,bdnm->bckm", tables[0], signal.reshape(pulse_rows, 2, outer_size, FACTOR)
    )
    real_part, imag_part = rotate_by(mixed_rows[:, 0], mixed_rows[:, 1], tables[2], -1.0)
    rotated = jnp.stack([real_part, imag_part], axis=1).astype(jnp.bfloat16)
    spectral = contract("bdkn,dnem->bkem", rotated, tables[1])
    filtered = matched(spectral, spectrum)
    returned = contract("bkdn,dnem->bkem", filtered, tables[4])
    real_part, imag_part = rotate_by(returned[:, :, 0], returned[:, :, 1], tables[2], 1.0)
    turned = jnp.stack([real_part, imag_part], axis=1).astype(jnp.bfloat16)
    lines = (contract("cmek,bekq->bcmq", tables[3], turned) * (1.0 / RANGE_BINS)).astype(
        jnp.bfloat16
    )
    return lines.reshape(pulse_rows, 2, RANGE_BINS)


def build_migration(coefficients, offsets):
    columns = jnp.arange(BAND_BINS + 2 * MARGIN_BINS, dtype=jnp.int32)[None, None, :, None]
    targets = (
        jnp.arange(BAND_BINS, dtype=jnp.int32)[None, :, None, None] + offsets[:, None, None, :]
    )
    migration_table = jnp.zeros(
        (coefficients.shape[0], BAND_BINS, BAND_BINS + 2 * MARGIN_BINS, coefficients.shape[3]),
        jnp.float32,
    )
    for tap_index in range(KERNEL):
        weights = coefficients[:, tap_index, :, None, :].astype(jnp.float32)
        migration_table = migration_table + jnp.where(
            columns == targets + tap_index, weights, jnp.zeros((), jnp.float32)
        )
    return migration_table.astype(jnp.bfloat16)


def migrate(padded, migration_table):
    range_rows = padded.shape[3] - 2 * MARGIN_BINS
    band_count = range_rows // BAND_BINS
    lead = padded.shape[:3]
    head_rows = padded[..., :range_rows].reshape(lead + (band_count, BAND_BINS))
    tail_rows = padded[..., BAND_BINS : BAND_BINS + range_rows].reshape(
        lead + (band_count, BAND_BINS)
    )
    window = jnp.concatenate([head_rows, tail_rows], axis=4)
    shifted = contract("jitg,kcgjt->kcgji", migration_table, window)
    return shifted.reshape(lead + (range_rows,))


def focus_azimuth(turned, migration_table, band_spectra, tables):
    range_rows = turned.shape[2]
    outer_size = PULSES // FACTOR
    signal = turned.reshape(outer_size, FACTOR, 2, range_rows)
    mixed_rows = contract("ckdn,nmdr->kmcr", tables[0], signal)
    twist = tables[2][:, :, None]
    real_part, imag_part = rotate_by(mixed_rows[:, :, 0], mixed_rows[:, :, 1], twist, -1.0)
    rotated = jnp.stack([real_part, imag_part], axis=2).astype(jnp.bfloat16)
    spectral = contract("kndr,dnem->kemr", rotated, tables[1]).astype(jnp.bfloat16)
    padded = extended(spectral, ((("section", "band"), 3),), MARGIN_BINS)
    moved = migrate(padded, migration_table)
    real_part = moved[:, 0]
    imag_part = moved[:, 1]
    spec_real = band_spectra[:, 0]
    spec_imag = band_spectra[:, 1]
    filtered = jnp.stack(
        [
            real_part * spec_real + imag_part * spec_imag,
            imag_part * spec_real - real_part * spec_imag,
        ],
        axis=1,
    ).astype(jnp.bfloat16)
    returned = contract("kdnr,dnem->kemr", filtered, tables[4])
    real_part, imag_part = rotate_by(returned[:, 0], returned[:, 1], twist, 1.0)
    back = jnp.stack([real_part, imag_part], axis=1).astype(jnp.bfloat16)
    focused = (contract("cmek,keqr->rcmq", tables[3], back) * (1.0 / PULSES)).astype(jnp.bfloat16)
    return focused.reshape(range_rows, 2, PULSES)


def corner_turn(compressed):
    pulse_rows = compressed.shape[0]
    block_count = compressed.shape[1]
    sections = lax.axis_size("section")
    band_count = lax.axis_size("band")
    local_rows = RANGE_BINS // (sections * band_count)
    shaped = compressed.reshape(1, 1, pulse_rows, block_count, 2, sections, band_count, local_rows)
    across_bands = lax.all_to_all(shaped, "band", split_axis=6, concat_axis=0, tiled=True)
    across_sections = lax.all_to_all(
        across_bands, "section", split_axis=5, concat_axis=1, tiled=True
    )
    arrived = across_sections.reshape(
        band_count * sections * pulse_rows, block_count, 2, local_rows
    )
    return arrived


def compress_send_kernel(
    axes,
    x_ref,
    left_ref,
    right_ref,
    right_back_ref,
    left_back_ref,
    cosine_ref,
    sine_ref,
    spec_real_ref,
    spec_imag_ref,
    arrived_ref,
    outbox,
    send_sem,
    recv_sem,
    local_sem,
):
    (major, major_size), (minor, minor_size) = axes
    count = major_size * minor_size
    step = pl.program_id(0)
    steps = pl.num_programs(0)
    pairs = outbox.shape[2]
    per_block = arrived_ref.shape[2] // pairs
    block = step // per_block
    first = (step % per_block) * pairs
    me = lax.axis_index(major) * minor_size + lax.axis_index(minor)
    source = lax.axis_index(minor) * major_size + lax.axis_index(major)

    @pl.when(step == 0)
    def _():
        barrier = pltpu.get_barrier_semaphore()

        def greet(k, carry):
            other = (me + k) % count
            pl.semaphore_signal(
                barrier,
                inc=1,
                device_id={major: other // minor_size, minor: other % minor_size},
                device_id_type=pl.DeviceIdType.MESH,
            )
            return carry

        lax.fori_loop(1, count, greet, 0)
        pl.semaphore_wait(barrier, count - 1)

    left = left_ref[...]
    right = right_ref[...]
    right_back = right_back_ref[...]
    left_back = left_back_ref[...]
    half = FACTOR

    def one_pair(pair, carry):
        cosine = cosine_ref[...]
        sine = sine_ref[...]
        spec_real = spec_real_ref[...]
        spec_imag = spec_imag_ref[...]
        signal = jnp.concatenate([x_ref[0, 2 * pair], x_ref[0, 2 * pair + 1]], axis=1)
        mixed = jnp.dot(left, signal, preferred_element_type=jnp.float32)
        rows = []
        for p in range(2):
            lanes = slice(p * half, (p + 1) * half)
            re, im = mixed[:half, lanes], mixed[half:, lanes]
            rows.append(
                jnp.concatenate([re * cosine + im * sine, im * cosine - re * sine], axis=1).astype(
                    jnp.bfloat16
                )
            )
        spectral = jnp.dot(
            jnp.concatenate(rows, axis=0), right, preferred_element_type=jnp.float32
        )
        rows = []
        for p in range(2):
            part = spectral[p * half : (p + 1) * half]
            re, im = part[:, :half], part[:, half:]
            rows.append(
                jnp.concatenate(
                    [re * spec_real + im * spec_imag, im * spec_real - re * spec_imag], axis=1
                ).astype(jnp.bfloat16)
            )
        returned = jnp.dot(
            jnp.concatenate(rows, axis=0), right_back, preferred_element_type=jnp.float32
        )
        columns = []
        for p in range(2):
            part = returned[p * half : (p + 1) * half]
            re, im = part[:, :half], part[:, half:]
            columns.append(
                jnp.concatenate([re * cosine - im * sine, re * sine + im * cosine], axis=0).astype(
                    jnp.bfloat16
                )
            )
        lines = jnp.dot(
            left_back, jnp.concatenate(columns, axis=1), preferred_element_type=jnp.float32
        ) * (1.0 / RANGE_BINS)
        tile = lines.shape[0] // count
        packed = jnp.concatenate(
            [
                lines[:, :half].reshape(count, tile, half),
                lines[:, half:].reshape(count, tile, half),
            ],
            axis=1,
        ).astype(jnp.bfloat16)
        outbox[step, :, pair] = packed
        return carry

    lax.fori_loop(0, pairs, one_pair, 0)

    own = pltpu.make_async_copy(
        outbox.at[step, me], arrived_ref.at[block, source, pl.ds(first, pairs)], local_sem
    )
    own.start()

    def post(k, carry):
        other = (me + k * 11) % count
        pltpu.make_async_remote_copy(
            src_ref=outbox.at[step, other],
            dst_ref=arrived_ref.at[block, source, pl.ds(first, pairs)],
            send_sem=send_sem,
            recv_sem=recv_sem,
            device_id={major: other // minor_size, minor: other % minor_size},
            device_id_type=pl.DeviceIdType.MESH,
        ).start()
        return carry

    lax.fori_loop(1, count, post, 0)
    own.wait()

    @pl.when(step == steps - 1)
    def _():
        whole = arrived_ref.at[:, pl.ds(0, count - 1)]
        pltpu.make_async_copy(whole, whole, send_sem).wait()
        pltpu.make_async_copy(whole, whole, recv_sem).wait()


def compress_and_turn(echoes, spectrum, axes):
    blocks, pulses, _, length = echoes.shape
    count = axes[0][1] * axes[1][1]
    outer_size = length // FACTOR
    rows_each = outer_size // count
    chunk = 16
    signal = (
        echoes.reshape(blocks, pulses, 2, outer_size, FACTOR)
        .transpose(0, 1, 3, 2, 4)
        .reshape(blocks, pulses, 2 * outer_size, FACTOR)
    )
    tables = make_tables(length)
    left = tables[0].transpose(0, 1, 3, 2).reshape(2 * outer_size, 2 * outer_size)
    right = tables[1].reshape(2 * FACTOR, 2 * FACTOR)
    right_back = tables[4].reshape(2 * FACTOR, 2 * FACTOR)
    left_back = (
        tables[3]
        .reshape(2, count, rows_each, 2 * outer_size)
        .transpose(1, 0, 2, 3)
        .reshape(2 * outer_size, 2 * outer_size)
    )
    steps_per_block = pulses // chunk
    steps = blocks * steps_per_block
    pairs = chunk // 2
    tile = 4 * rows_each

    def whole(array):
        return pl.BlockSpec(array.shape, lambda s: (0,) * array.ndim)

    operands = (
        left,
        right,
        right_back,
        left_back,
        jnp.cos(tables[2]),
        jnp.sin(tables[2]),
        spectrum[:, 0],
        spectrum[:, 1],
    )
    return pl.pallas_call(
        functools.partial(compress_send_kernel, axes),
        grid=(steps,),
        in_specs=[
            pl.BlockSpec(
                (1, chunk, 2 * outer_size, FACTOR),
                lambda s: (s // steps_per_block, s % steps_per_block, 0, 0),
            )
        ]
        + [whole(array) for array in operands],
        out_specs=pl.BlockSpec(memory_space=pl.ANY),
        out_shape=jax.ShapeDtypeStruct(
            (blocks, count, pulses // 2, tile, FACTOR), jnp.bfloat16
        ),
        scratch_shapes=[
            pltpu.VMEM((steps, count, pairs, tile, FACTOR), jnp.bfloat16),
            pltpu.SemaphoreType.DMA,
            pltpu.SemaphoreType.DMA,
            pltpu.SemaphoreType.DMA,
        ],
        compiler_params=pltpu.CompilerParams(
            collective_id=0, has_side_effects=True, vmem_limit_bytes=44 * 2**20
        ),
        cost_estimate=pl.CostEstimate(
            flops=blocks * pulses * 16 * FACTOR**2 * 2 * FACTOR,
            bytes_accessed=4 * echoes.size,
            transcendentals=0,
        ),
        name="compress_turn",
    )(signal, *operands)


def forward_kernel(
    order_ref, x_ref, cosine_ref, sine_ref, left_ref, right_ref, out_ref, lifted, mixed, spread
):
    step = pl.program_id(1)
    chunk = x_ref.shape[2]
    outer_size = x_ref.shape[1]
    tile = x_ref.shape[3]
    tiles = mixed.shape[0]
    rows = 2 * outer_size
    chunks = FACTOR // (2 * chunk)

    @pl.when(step < chunks)
    def _():
        lifted[...] = x_ref[0].reshape(outer_size * chunk * tile, FACTOR).astype(jnp.float32)
        left = left_ref[...]

        def one_column(n, carry):
            base = n * (tile // 2)
            parts = []
            for j in range(tiles):
                parts.append(
                    jnp.concatenate(
                        [
                            lifted[pl.ds(base + c * tiles + j, outer_size, stride=chunk * tile), :]
                            for c in range(2)
                        ],
                        axis=0,
                    )
                )
            signal = jnp.concatenate(parts, axis=1).astype(jnp.bfloat16)
            product = jnp.dot(left, signal, preferred_element_type=jnp.float32)
            cosine, sine = cosine_ref[n], sine_ref[n]
            start = pl.multiple_of((step * 2 * chunk + n) * rows, rows)
            for j in range(tiles):
                lanes = slice(j * FACTOR, (j + 1) * FACTOR)
                re, im = product[:outer_size, lanes], product[outer_size:, lanes]
                mixed[j, pl.ds(start, outer_size), :] = re * cosine + im * sine
                mixed[j, pl.ds(start + outer_size, outer_size), :] = im * cosine - re * sine
            return carry

        lax.fori_loop(0, 2 * chunk, one_column, 0)

    @pl.when(step >= chunks)
    def _():
        right = right_ref[...]
        j = jnp.maximum(step - chunks, 0)

        def one_row(k, carry):
            signal = jnp.concatenate(
                [mixed[j, pl.ds(k + c * outer_size, FACTOR, stride=rows), :] for c in range(2)],
                axis=0,
            ).astype(jnp.bfloat16)
            product = jnp.dot(right, signal, preferred_element_type=jnp.float32)
            for c in range(2):
                spread[pl.ds(k + c * outer_size, FACTOR, stride=rows), :] = product[
                    c * FACTOR : (c + 1) * FACTOR
                ]
            return carry

        lax.fori_loop(0, outer_size, one_row, 0)
        out_ref[0] = spread[...].reshape(FACTOR, rows, FACTOR).astype(jnp.bfloat16)


def forward_azimuth(arrived, block_order, tables):
    blocks, outer_size, pairs, tile, _ = arrived.shape
    tiles = tile // 4
    rows = 2 * outer_size
    chunk = 8
    chunks = pairs // chunk
    left = tables[0].reshape(rows, rows)
    right = tables[1].reshape(2 * FACTOR, 2 * FACTOR).T
    cosine = jnp.broadcast_to(jnp.cos(tables[2]).T[:, :, None], (FACTOR, outer_size, FACTOR))
    sine = jnp.broadcast_to(jnp.sin(tables[2]).T[:, :, None], (FACTOR, outer_size, FACTOR))
    twist = pl.BlockSpec(
        (2 * chunk, outer_size, FACTOR), lambda b, s, order: (jnp.minimum(s, chunks - 1), 0, 0)
    )
    return pl.pallas_call(
        forward_kernel,
        grid_spec=pltpu.PrefetchScalarGridSpec(
            num_scalar_prefetch=1,
            grid=(blocks, chunks + tiles),
            in_specs=[
                pl.BlockSpec(
                    (1, outer_size, chunk, tile, FACTOR),
                    lambda b, s, order: (order[b], 0, jnp.minimum(s, chunks - 1), 0, 0),
                ),
                twist,
                twist,
                pl.BlockSpec(left.shape, lambda b, s, order: (0, 0)),
                pl.BlockSpec(right.shape, lambda b, s, order: (0, 0)),
            ],
            out_specs=pl.BlockSpec(
                (1, FACTOR, rows, FACTOR),
                lambda b, s, order: (b, 0, 0, jnp.maximum(s - chunks, 0)),
            ),
            scratch_shapes=[
                pltpu.VMEM((outer_size * chunk * tile, FACTOR), jnp.float32),
                pltpu.VMEM((tiles, FACTOR * rows, FACTOR), jnp.float32),
                pltpu.VMEM((FACTOR * rows, FACTOR), jnp.float32),
            ],
        ),
        out_shape=jax.ShapeDtypeStruct((blocks, FACTOR, rows, tiles * FACTOR), jnp.bfloat16),
        compiler_params=pltpu.CompilerParams(vmem_limit_bytes=44 * 2**20),
        name="azimuth_forward",
    )(block_order, arrived, cosine, sine, left, right)


def back_kernel(
    here_ref,
    before_ref,
    after_ref,
    halo_ref,
    coefficient_ref,
    offset_ref,
    spectra_ref,
    right_ref,
    left_ref,
    cosine_ref,
    sine_ref,
    out_ref,
    filtered,
    turned,
):
    tile = pl.program_id(0)
    step = pl.program_id(1)
    blocks, groups, rows, _ = here_ref.shape
    outer_size = rows // 2
    chunks = FACTOR // groups
    last = pl.num_programs(0) - 1

    @pl.when(step < chunks)
    def _():
        row = lax.broadcasted_iota(jnp.int32, (2 * FACTOR, FACTOR), 0)
        lane = lax.broadcasted_iota(jnp.int32, (2 * FACTOR, FACTOR), 1)
        spot = jnp.where(
            row < FACTOR + BAND_BINS, row, jnp.where(row < 2 * FACTOR, row - 2 * FACTOR, row)
        )
        spot = jnp.where(row < FACTOR, row, spot)
        column = spot + MARGIN_BINS - lane
        side = lax.broadcasted_iota(jnp.int32, (rows, FACTOR), 1)

        def one_group(g, carry):
            gap = column - offset_ref[0, pl.ds(g, 1), :]
            taps = coefficient_ref[0, g]
            table = jnp.zeros((2 * FACTOR, FACTOR), jnp.float32)
            for s in range(KERNEL):
                table = jnp.where(gap == s, taps[s : s + 1, :], table)
            table = table.astype(jnp.bfloat16)
            windows = []
            for b in range(blocks):
                halo = halo_ref[b, g].astype(jnp.float32)
                after = jnp.where(tile == last, halo, after_ref[b, g].astype(jnp.float32))
                before = jnp.where(tile == 0, halo, before_ref[b, g].astype(jnp.float32))
                edges = jnp.where(side < BAND_BINS, after, before).astype(jnp.bfloat16)
                windows.append(jnp.concatenate([here_ref[b, g], edges], axis=1))
            moved = jnp.dot(
                jnp.concatenate(windows, axis=0), table, preferred_element_type=jnp.float32
            )
            spec_real, spec_imag = spectra_ref[0, g, :outer_size], spectra_ref[0, g, outer_size:]
            start = pl.multiple_of((step * groups + g) * rows, rows)
            for b in range(blocks):
                re = moved[b * rows : b * rows + outer_size]
                im = moved[b * rows + outer_size : (b + 1) * rows]
                filtered[b, pl.ds(start, outer_size), :] = re * spec_real + im * spec_imag
                filtered[b, pl.ds(start + outer_size, outer_size), :] = (
                    im * spec_real - re * spec_imag
                )
            return carry

        lax.fori_loop(0, groups, one_group, 0)

    @pl.when(step >= chunks)
    def _():
        b = jnp.maximum(step - chunks, 0)
        right = right_ref[...]
        left = left_ref[...]

        def one_row(k, carry):
            signal = jnp.concatenate(
                [filtered[b, pl.ds(k + c * outer_size, FACTOR, stride=rows), :] for c in range(2)],
                axis=0,
            ).astype(jnp.bfloat16)
            returned = lax.dot_general(
                signal, right, (((0,), (0,)), ((), ())), preferred_element_type=jnp.float32
            )
            cosine, sine = cosine_ref[pl.ds(k, 1), :], sine_ref[pl.ds(k, 1), :]
            re, im = returned[:, :FACTOR], returned[:, FACTOR:]
            turned[pl.ds(k, FACTOR, stride=rows), :] = re * cosine - im * sine
            turned[pl.ds(k + outer_size, FACTOR, stride=rows), :] = re * sine + im * cosine
            return carry

        lax.fori_loop(0, outer_size, one_row, 0)
        wide = left.shape[0]
        each = wide // rows

        def some_bins(r, carry):
            start = pl.multiple_of(r * wide, wide)
            signal = turned[pl.ds(start, wide), :].astype(jnp.bfloat16)
            lines = jnp.dot(left, signal, preferred_element_type=jnp.float32) * (1.0 / PULSES)
            out_ref[0, pl.ds(r * each, each)] = lines.reshape(each, rows, FACTOR).astype(
                jnp.bfloat16
            )
            return carry

        lax.fori_loop(0, FACTOR // each, some_bins, 0)


def back_azimuth(spectral, halo, spectra, coefficients, offsets, tables):
    blocks, _, rows, width = spectral.shape
    tiles = width // FACTOR
    outer_size = rows // 2
    groups = 8
    chunks = FACTOR // groups
    per_tile = FACTOR // BAND_BINS
    taps = (
        coefficients.reshape(tiles, per_tile, KERNEL, BAND_BINS, FACTOR)
        .transpose(0, 4, 2, 1, 3)
        .reshape(tiles, FACTOR, KERNEL, FACTOR)
        .astype(jnp.float32)
    )
    shifts = jnp.repeat(
        offsets.reshape(tiles, per_tile, FACTOR).transpose(0, 2, 1), BAND_BINS, axis=2
    )
    doppler = jnp.repeat(
        spectra.reshape(tiles, per_tile, outer_size, 2, FACTOR)
        .transpose(0, 4, 3, 2, 1)
        .reshape(tiles, FACTOR, rows, per_tile),
        BAND_BINS,
        axis=3,
    )
    right = tables[4].reshape(2 * FACTOR, 2 * FACTOR)
    small = tables[3].transpose(1, 0, 2, 3).reshape(rows, rows)
    left = jnp.kron(jnp.eye(2 * FACTOR // rows, dtype=jnp.float32), small.astype(jnp.float32))
    left = left.astype(jnp.bfloat16)

    def at(s):
        return jnp.minimum(s, chunks - 1)

    def piece(shift):
        return pl.BlockSpec(
            (blocks, groups, rows, FACTOR),
            lambda t, s: (0, at(s), 0, jnp.clip(t + shift, 0, tiles - 1)),
        )

    def whole(array):
        return pl.BlockSpec(array.shape, lambda t, s: (0,) * array.ndim)

    cosine, sine = jnp.cos(tables[2]), jnp.sin(tables[2])
    image = pl.pallas_call(
        back_kernel,
        grid=(tiles, chunks + blocks),
        in_specs=[
            piece(0),
            piece(-1),
            piece(1),
            pl.BlockSpec((blocks, groups, rows, FACTOR), lambda t, s: (0, at(s), 0, 0)),
            pl.BlockSpec((1, groups, KERNEL, FACTOR), lambda t, s: (t, at(s), 0, 0)),
            pl.BlockSpec((1, groups, FACTOR), lambda t, s: (t, at(s), 0)),
            pl.BlockSpec((1, groups, rows, FACTOR), lambda t, s: (t, at(s), 0, 0)),
            whole(right),
            whole(left),
            whole(cosine),
            whole(sine),
        ],
        out_specs=pl.BlockSpec(
            (1, FACTOR, rows, FACTOR), lambda t, s: (jnp.maximum(s - chunks, 0), t, 0, 0)
        ),
        out_shape=jax.ShapeDtypeStruct((blocks, width, rows, FACTOR), jnp.bfloat16),
        scratch_shapes=[
            pltpu.VMEM((blocks, FACTOR * rows, FACTOR), jnp.float32),
            pltpu.VMEM((FACTOR * rows, FACTOR), jnp.float32),
        ],
        compiler_params=pltpu.CompilerParams(vmem_limit_bytes=44 * 2**20),
        name="azimuth_back",
    )(
        spectral,
        spectral,
        spectral,
        halo,
        taps,
        shifts,
        doppler,
        right,
        left,
        cosine,
        sine,
    )
    return (
        image.reshape(blocks, width, outer_size, 2, FACTOR)
        .transpose(0, 1, 3, 2, 4)
        .reshape(blocks, width, 2, outer_size * FACTOR)
    )


def halo_of(spectral):
    axes = ("section", "band")
    count = lax.axis_size(axes)
    up = [(i, i + 1) for i in range(count - 1)]
    down = [(i + 1, i) for i in range(count - 1)]
    width = spectral.shape[3]
    before = lax.ppermute(spectral[..., width - MARGIN_BINS :], axes, up)
    after = lax.ppermute(spectral[..., :MARGIN_BINS], axes, down)
    middle = jnp.zeros(spectral.shape[:3] + (FACTOR - 2 * MARGIN_BINS,), spectral.dtype)
    return jnp.concatenate([after, middle, before], axis=3)


def on_device(echoes, replica, azimuth_taps, coefficients, offsets, block_order):
    sections = lax.axis_size("section")
    bands = lax.axis_size("band")
    count = sections * bands
    direct = (RANGE_BINS // FACTOR) == 4 * count and echoes.shape[1] % 16 == 0
    range_tables = make_tables(RANGE_BINS)
    pulse_tables = make_tables(PULSES)
    range_spectrum = exact_spectrum(replica[None], RANGE_BINS)[0]
    spectra = exact_spectrum(azimuth_taps, PULSES)
    if direct:
        arrived = compress_and_turn(
            echoes, range_spectrum, (("section", sections), ("band", bands))
        )
        spectral = forward_azimuth(arrived, block_order, pulse_tables)
        return back_azimuth(
            spectral, halo_of(spectral), spectra, coefficients, offsets, pulse_tables
        )
    band_spectra = jnp.repeat(jnp.transpose(spectra, (1, 2, 3, 0)), BAND_BINS, axis=3)
    migration_table = build_migration(coefficients, offsets)
    images = []
    for position in range(BLOCKS):
        signal = lax.dynamic_index_in_dim(echoes, block_order[position], 0, keepdims=False)
        compressed = compress_range(signal, range_spectrum, range_tables)
        turned = corner_turn(compressed[:, None])
        images.append(focus_azimuth(turned[:, 0], migration_table, band_spectra, pulse_tables))
    return jnp.stack(images, axis=0)


def solution(mesh):
    in_specs = (
        P(None, ("band", "section"), None, None),
        P(),
        P(("section", "band"), None, None),
        P(("section", "band"), None, None, None),
        P(("section", "band"), None),
        P(),
    )
    out_specs = P(None, ("section", "band"), None, None)
    return jax.shard_map(
        on_device, mesh=mesh, in_specs=in_specs, out_specs=out_specs, check_vma=False
    )
```

```python
import functools
import math

import jax
import jax.numpy as jnp
from jax import lax
from jax.experimental import pallas as pl
from jax.experimental.pallas import tpu as pltpu
from jax.sharding import PartitionSpec as P

RANGE_BINS = 16384
PULSES = 4096
FACTOR = 128
BAND_BINS = 64
MARGIN_BINS = 32
KERNEL = 8
BLOCKS = 2


def extended(cells, sides, width):
    for axis, dim in sides:
        count = lax.axis_size(axis)
        ends = count - 1
        head = lax.slice_in_dim(cells, 0, width, axis=dim)
        tail = lax.slice_in_dim(cells, cells.shape[dim] - width, cells.shape[dim], axis=dim)
        cells = jnp.concatenate(
            [
                lax.ppermute(tail, axis, [(i, (i + 1) % count) for i in range(ends)]),
                cells,
                lax.ppermute(head, axis, [((i + 1) % count, i) for i in range(ends)]),
            ],
            axis=dim,
        )
    return cells


def phases(outer_size, inner_size, length):
    outer_index = jnp.arange(outer_size, dtype=jnp.int32)[:, None]
    inner_index = jnp.arange(inner_size, dtype=jnp.int32)[None, :]
    return 2.0 * math.pi / length * (outer_index * inner_index % length).astype(jnp.float32)


def left_matrix(phase_table, signum):
    cosine = jnp.cos(phase_table)
    sine_part = signum * jnp.sin(phase_table)
    upper_rows = jnp.stack([cosine, -sine_part], axis=1)
    lower_rows = jnp.stack([sine_part, cosine], axis=1)
    return jnp.stack([upper_rows, lower_rows], axis=0)


def right_matrix(phase_table, signum):
    cosine = jnp.cos(phase_table)
    sine_part = signum * jnp.sin(phase_table)
    leading = jnp.stack([cosine, sine_part], axis=1)
    trailing = jnp.stack([-sine_part, cosine], axis=1)
    return jnp.stack([leading, trailing], axis=0)


def rotate_by(real_part, imag_part, phase_table, signum):
    cosine = jnp.cos(phase_table)
    sine_part = signum * jnp.sin(phase_table)
    return (real_part * cosine - imag_part * sine_part, real_part * sine_part + imag_part * cosine)


def make_tables(length):
    outer_size = length // FACTOR
    outer_phase = phases(outer_size, outer_size, outer_size)
    inner_phase = phases(FACTOR, FACTOR, FACTOR)
    twist_phase = phases(outer_size, FACTOR, length)
    return (
        left_matrix(outer_phase, -1.0).astype(jnp.bfloat16),
        right_matrix(inner_phase, -1.0).astype(jnp.bfloat16),
        twist_phase,
        left_matrix(outer_phase, 1.0).astype(jnp.bfloat16),
        right_matrix(inner_phase, 1.0).astype(jnp.bfloat16),
    )


def contract(pattern, left_side, right_side):
    return jnp.einsum(pattern, left_side, right_side, preferred_element_type=jnp.float32)


def exact_spectrum(tap_rows, length):
    outer_size = length // FACTOR
    padded = jnp.pad(tap_rows, ((0, 0), (0, 0), (0, length - tap_rows.shape[2])))
    padded = padded.reshape(tap_rows.shape[0], 2, outer_size, FACTOR)
    outer_phase = phases(outer_size, outer_size, outer_size)
    inner_phase = phases(FACTOR, FACTOR, FACTOR)
    twist_phase = phases(outer_size, FACTOR, length)
    mixed_rows = jnp.einsum(
        "ckdn,bdnm->bckm", left_matrix(outer_phase, -1.0), padded, precision=lax.Precision.HIGHEST
    )
    real_part, imag_part = rotate_by(mixed_rows[:, 0], mixed_rows[:, 1], twist_phase, -1.0)
    rotated = jnp.stack([real_part, imag_part], axis=1)
    return jnp.einsum(
        "bdkn,dnem->bkem", rotated, right_matrix(inner_phase, -1.0), precision=lax.Precision.HIGHEST
    )


def matched(values, spectrum):
    real_part = values[..., 0, :]
    imag_part = values[..., 1, :]
    spec_real = spectrum[..., 0, :]
    spec_imag = spectrum[..., 1, :]
    return jnp.stack(
        [
            real_part * spec_real + imag_part * spec_imag,
            imag_part * spec_real - real_part * spec_imag,
        ],
        axis=-2,
    ).astype(jnp.bfloat16)


def compress_range(signal, spectrum, tables):
    pulse_rows = signal.shape[0]
    outer_size = RANGE_BINS // FACTOR
    mixed_rows = contract(
        "ckdn,bdnm->bckm", tables[0], signal.reshape(pulse_rows, 2, outer_size, FACTOR)
    )
    real_part, imag_part = rotate_by(mixed_rows[:, 0], mixed_rows[:, 1], tables[2], -1.0)
    rotated = jnp.stack([real_part, imag_part], axis=1).astype(jnp.bfloat16)
    spectral = contract("bdkn,dnem->bkem", rotated, tables[1])
    filtered = matched(spectral, spectrum)
    returned = contract("bkdn,dnem->bkem", filtered, tables[4])
    real_part, imag_part = rotate_by(returned[:, :, 0], returned[:, :, 1], tables[2], 1.0)
    turned = jnp.stack([real_part, imag_part], axis=1).astype(jnp.bfloat16)
    lines = (contract("cmek,bekq->bcmq", tables[3], turned) * (1.0 / RANGE_BINS)).astype(
        jnp.bfloat16
    )
    return lines.reshape(pulse_rows, 2, RANGE_BINS)


def build_migration(coefficients, offsets):
    columns = jnp.arange(BAND_BINS + 2 * MARGIN_BINS, dtype=jnp.int32)[None, None, :, None]
    targets = (
        jnp.arange(BAND_BINS, dtype=jnp.int32)[None, :, None, None] + offsets[:, None, None, :]
    )
    migration_table = jnp.zeros(
        (coefficients.shape[0], BAND_BINS, BAND_BINS + 2 * MARGIN_BINS, coefficients.shape[3]),
        jnp.float32,
    )
    for tap_index in range(KERNEL):
        weights = coefficients[:, tap_index, :, None, :].astype(jnp.float32)
        migration_table = migration_table + jnp.where(
            columns == targets + tap_index, weights, jnp.zeros((), jnp.float32)
        )
    return migration_table.astype(jnp.bfloat16)


def migrate(padded, migration_table):
    range_rows = padded.shape[3] - 2 * MARGIN_BINS
    band_count = range_rows // BAND_BINS
    lead = padded.shape[:3]
    head_rows = padded[..., :range_rows].reshape(lead + (band_count, BAND_BINS))
    tail_rows = padded[..., BAND_BINS : BAND_BINS + range_rows].reshape(
        lead + (band_count, BAND_BINS)
    )
    window = jnp.concatenate([head_rows, tail_rows], axis=4)
    shifted = contract("jitg,kcgjt->kcgji", migration_table, window)
    return shifted.reshape(lead + (range_rows,))


def focus_azimuth(turned, migration_table, band_spectra, tables):
    range_rows = turned.shape[2]
    outer_size = PULSES // FACTOR
    signal = turned.reshape(outer_size, FACTOR, 2, range_rows)
    mixed_rows = contract("ckdn,nmdr->kmcr", tables[0], signal)
    twist = tables[2][:, :, None]
    real_part, imag_part = rotate_by(mixed_rows[:, :, 0], mixed_rows[:, :, 1], twist, -1.0)
    rotated = jnp.stack([real_part, imag_part], axis=2).astype(jnp.bfloat16)
    spectral = contract("kndr,dnem->kemr", rotated, tables[1]).astype(jnp.bfloat16)
    padded = extended(spectral, ((("section", "band"), 3),), MARGIN_BINS)
    moved = migrate(padded, migration_table)
    real_part = moved[:, 0]
    imag_part = moved[:, 1]
    spec_real = band_spectra[:, 0]
    spec_imag = band_spectra[:, 1]
    filtered = jnp.stack(
        [
            real_part * spec_real + imag_part * spec_imag,
            imag_part * spec_real - real_part * spec_imag,
        ],
        axis=1,
    ).astype(jnp.bfloat16)
    returned = contract("kdnr,dnem->kemr", filtered, tables[4])
    real_part, imag_part = rotate_by(returned[:, 0], returned[:, 1], twist, 1.0)
    back = jnp.stack([real_part, imag_part], axis=1).astype(jnp.bfloat16)
    focused = (contract("cmek,keqr->rcmq", tables[3], back) * (1.0 / PULSES)).astype(jnp.bfloat16)
    return focused.reshape(range_rows, 2, PULSES)


def corner_turn(compressed):
    pulse_rows = compressed.shape[0]
    block_count = compressed.shape[1]
    sections = lax.axis_size("section")
    band_count = lax.axis_size("band")
    local_rows = RANGE_BINS // (sections * band_count)
    shaped = compressed.reshape(1, 1, pulse_rows, block_count, 2, sections, band_count, local_rows)
    across_bands = lax.all_to_all(shaped, "band", split_axis=6, concat_axis=0, tiled=True)
    across_sections = lax.all_to_all(
        across_bands, "section", split_axis=5, concat_axis=1, tiled=True
    )
    arrived = across_sections.reshape(
        band_count * sections * pulse_rows, block_count, 2, local_rows
    )
    return arrived


def compress_send_kernel(
    axes,
    x_ref,
    left_ref,
    right_ref,
    right_back_ref,
    left_back_ref,
    cosine_ref,
    sine_ref,
    spec_real_ref,
    spec_imag_ref,
    arrived_ref,
    outbox,
    send_sem,
    recv_sem,
    local_sem,
):
    (major, major_size), (minor, minor_size) = axes
    count = major_size * minor_size
    step = pl.program_id(0)
    steps = pl.num_programs(0)
    pairs = outbox.shape[2]
    per_block = arrived_ref.shape[2] // pairs
    block = step // per_block
    first = (step % per_block) * pairs
    me = lax.axis_index(major) * minor_size + lax.axis_index(minor)
    source = lax.axis_index(minor) * major_size + lax.axis_index(major)

    @pl.when(step == 0)
    def _():
        barrier = pltpu.get_barrier_semaphore()

        def greet(k, carry):
            other = (me + k) % count
            pl.semaphore_signal(
                barrier,
                inc=1,
                device_id={major: other // minor_size, minor: other % minor_size},
                device_id_type=pl.DeviceIdType.MESH,
            )
            return carry

        lax.fori_loop(1, count, greet, 0)
        pl.semaphore_wait(barrier, count - 1)

    left = left_ref[...]
    right = right_ref[...]
    right_back = right_back_ref[...]
    left_back = left_back_ref[...]
    half = FACTOR

    def one_pair(pair, carry):
        cosine = cosine_ref[...]
        sine = sine_ref[...]
        spec_real = spec_real_ref[...]
        spec_imag = spec_imag_ref[...]
        signal = jnp.concatenate([x_ref[0, 2 * pair], x_ref[0, 2 * pair + 1]], axis=1)
        mixed = jnp.dot(left, signal, preferred_element_type=jnp.float32)
        rows = []
        for p in range(2):
            lanes = slice(p * half, (p + 1) * half)
            re, im = mixed[:half, lanes], mixed[half:, lanes]
            rows.append(
                jnp.concatenate([re * cosine + im * sine, im * cosine - re * sine], axis=1).astype(
                    jnp.bfloat16
                )
            )
        spectral = jnp.dot(
            jnp.concatenate(rows, axis=0), right, preferred_element_type=jnp.float32
        )
        rows = []
        for p in range(2):
            part = spectral[p * half : (p + 1) * half]
            re, im = part[:, :half], part[:, half:]
            rows.append(
                jnp.concatenate(
                    [re * spec_real + im * spec_imag, im * spec_real - re * spec_imag], axis=1
                ).astype(jnp.bfloat16)
            )
        returned = jnp.dot(
            jnp.concatenate(rows, axis=0), right_back, preferred_element_type=jnp.float32
        )
        columns = []
        for p in range(2):
            part = returned[p * half : (p + 1) * half]
            re, im = part[:, :half], part[:, half:]
            columns.append(
                jnp.concatenate([re * cosine - im * sine, re * sine + im * cosine], axis=0).astype(
                    jnp.bfloat16
                )
            )
        lines = jnp.dot(
            left_back, jnp.concatenate(columns, axis=1), preferred_element_type=jnp.float32
        ) * (1.0 / RANGE_BINS)
        tile = lines.shape[0] // count
        packed = jnp.concatenate(
            [
                lines[:, :half].reshape(count, tile, half),
                lines[:, half:].reshape(count, tile, half),
            ],
            axis=1,
        ).astype(jnp.bfloat16)
        outbox[step, :, pair] = packed
        return carry

    lax.fori_loop(0, pairs, one_pair, 0)

    own = pltpu.make_async_copy(
        outbox.at[step, me], arrived_ref.at[block, source, pl.ds(first, pairs)], local_sem
    )
    own.start()

    def post(k, carry):
        other = (me + k * 11) % count
        pltpu.make_async_remote_copy(
            src_ref=outbox.at[step, other],
            dst_ref=arrived_ref.at[block, source, pl.ds(first, pairs)],
            send_sem=send_sem,
            recv_sem=recv_sem,
            device_id={major: other // minor_size, minor: other % minor_size},
            device_id_type=pl.DeviceIdType.MESH,
        ).start()
        return carry

    lax.fori_loop(1, count, post, 0)
    own.wait()

    @pl.when(step == steps - 1)
    def _():
        whole = arrived_ref.at[:, pl.ds(0, count - 1)]
        pltpu.make_async_copy(whole, whole, send_sem).wait()
        pltpu.make_async_copy(whole, whole, recv_sem).wait()


def compress_and_turn(echoes, spectrum, axes):
    blocks, pulses, _, length = echoes.shape
    count = axes[0][1] * axes[1][1]
    outer_size = length // FACTOR
    rows_each = outer_size // count
    chunk = 16
    signal = (
        echoes.reshape(blocks, pulses, 2, outer_size, FACTOR)
        .transpose(0, 1, 3, 2, 4)
        .reshape(blocks, pulses, 2 * outer_size, FACTOR)
    )
    tables = make_tables(length)
    left = tables[0].transpose(0, 1, 3, 2).reshape(2 * outer_size, 2 * outer_size)
    right = tables[1].reshape(2 * FACTOR, 2 * FACTOR)
    right_back = tables[4].reshape(2 * FACTOR, 2 * FACTOR)
    left_back = (
        tables[3]
        .reshape(2, count, rows_each, 2 * outer_size)
        .transpose(1, 0, 2, 3)
        .reshape(2 * outer_size, 2 * outer_size)
    )
    steps_per_block = pulses // chunk
    steps = blocks * steps_per_block
    pairs = chunk // 2
    tile = 4 * rows_each

    def whole(array):
        return pl.BlockSpec(array.shape, lambda s: (0,) * array.ndim)

    operands = (
        left,
        right,
        right_back,
        left_back,
        jnp.cos(tables[2]),
        jnp.sin(tables[2]),
        spectrum[:, 0],
        spectrum[:, 1],
    )
    return pl.pallas_call(
        functools.partial(compress_send_kernel, axes),
        grid=(steps,),
        in_specs=[
            pl.BlockSpec(
                (1, chunk, 2 * outer_size, FACTOR),
                lambda s: (s // steps_per_block, s % steps_per_block, 0, 0),
            )
        ]
        + [whole(array) for array in operands],
        out_specs=pl.BlockSpec(memory_space=pl.ANY),
        out_shape=jax.ShapeDtypeStruct(
            (blocks, count, pulses // 2, tile, FACTOR), jnp.bfloat16
        ),
        scratch_shapes=[
            pltpu.VMEM((steps, count, pairs, tile, FACTOR), jnp.bfloat16),
            pltpu.SemaphoreType.DMA,
            pltpu.SemaphoreType.DMA,
            pltpu.SemaphoreType.DMA,
        ],
        compiler_params=pltpu.CompilerParams(
            collective_id=0, has_side_effects=True, vmem_limit_bytes=44 * 2**20
        ),
        cost_estimate=pl.CostEstimate(
            flops=blocks * pulses * 16 * FACTOR**2 * 2 * FACTOR,
            bytes_accessed=4 * echoes.size,
            transcendentals=0,
        ),
        name="compress_turn",
    )(signal, *operands)


def forward_kernel(
    order_ref, x_ref, cosine_ref, sine_ref, left_ref, right_ref, out_ref, lifted, mixed, spread
):
    step = pl.program_id(1)
    chunk = x_ref.shape[2]
    outer_size = x_ref.shape[1]
    tile = x_ref.shape[3]
    tiles = mixed.shape[0]
    rows = 2 * outer_size
    chunks = FACTOR // (2 * chunk)

    @pl.when(step < chunks)
    def _():
        lifted[...] = x_ref[0].reshape(outer_size * chunk * tile, FACTOR).astype(jnp.float32)
        left = left_ref[...]

        def one_column(n, carry):
            base = n * (tile // 2)
            parts = []
            for j in range(tiles):
                parts.append(
                    jnp.concatenate(
                        [
                            lifted[pl.ds(base + c * tiles + j, outer_size, stride=chunk * tile), :]
                            for c in range(2)
                        ],
                        axis=0,
                    )
                )
            signal = jnp.concatenate(parts, axis=1).astype(jnp.bfloat16)
            product = jnp.dot(left, signal, preferred_element_type=jnp.float32)
            cosine, sine = cosine_ref[n], sine_ref[n]
            start = pl.multiple_of((step * 2 * chunk + n) * rows, rows)
            for j in range(tiles):
                lanes = slice(j * FACTOR, (j + 1) * FACTOR)
                re, im = product[:outer_size, lanes], product[outer_size:, lanes]
                mixed[j, pl.ds(start, outer_size), :] = re * cosine + im * sine
                mixed[j, pl.ds(start + outer_size, outer_size), :] = im * cosine - re * sine
            return carry

        lax.fori_loop(0, 2 * chunk, one_column, 0, unroll=4)

    @pl.when(step >= chunks)
    def _():
        right = right_ref[...]
        j = jnp.maximum(step - chunks, 0)

        def one_row(k, carry):
            signal = jnp.concatenate(
                [mixed[j, pl.ds(k + c * outer_size, FACTOR, stride=rows), :] for c in range(2)],
                axis=0,
            ).astype(jnp.bfloat16)
            product = jnp.dot(right, signal, preferred_element_type=jnp.float32)
            for c in range(2):
                spread[pl.ds(k + c * outer_size, FACTOR, stride=rows), :] = product[
                    c * FACTOR : (c + 1) * FACTOR
                ]
            return carry

        lax.fori_loop(0, outer_size, one_row, 0, unroll=4)
        out_ref[0] = spread[...].reshape(FACTOR, rows, FACTOR).astype(jnp.bfloat16)


def forward_azimuth(arrived, block_order, tables):
    blocks, outer_size, pairs, tile, _ = arrived.shape
    tiles = tile // 4
    rows = 2 * outer_size
    chunk = 8
    chunks = pairs // chunk
    left = tables[0].reshape(rows, rows)
    right = tables[1].reshape(2 * FACTOR, 2 * FACTOR).T
    cosine = jnp.broadcast_to(jnp.cos(tables[2]).T[:, :, None], (FACTOR, outer_size, FACTOR))
    sine = jnp.broadcast_to(jnp.sin(tables[2]).T[:, :, None], (FACTOR, outer_size, FACTOR))
    twist = pl.BlockSpec(
        (2 * chunk, outer_size, FACTOR), lambda b, s, order: (jnp.minimum(s, chunks - 1), 0, 0)
    )
    return pl.pallas_call(
        forward_kernel,
        grid_spec=pltpu.PrefetchScalarGridSpec(
            num_scalar_prefetch=1,
            grid=(blocks, chunks + tiles),
            in_specs=[
                pl.BlockSpec(
                    (1, outer_size, chunk, tile, FACTOR),
                    lambda b, s, order: (order[b], 0, jnp.minimum(s, chunks - 1), 0, 0),
                ),
                twist,
                twist,
                pl.BlockSpec(left.shape, lambda b, s, order: (0, 0)),
                pl.BlockSpec(right.shape, lambda b, s, order: (0, 0)),
            ],
            out_specs=pl.BlockSpec(
                (1, FACTOR, rows, FACTOR),
                lambda b, s, order: (b, 0, 0, jnp.maximum(s - chunks, 0)),
            ),
            scratch_shapes=[
                pltpu.VMEM((outer_size * chunk * tile, FACTOR), jnp.float32),
                pltpu.VMEM((tiles, FACTOR * rows, FACTOR), jnp.float32),
                pltpu.VMEM((FACTOR * rows, FACTOR), jnp.float32),
            ],
        ),
        out_shape=jax.ShapeDtypeStruct((blocks, FACTOR, rows, tiles * FACTOR), jnp.bfloat16),
        compiler_params=pltpu.CompilerParams(vmem_limit_bytes=44 * 2**20),
        name="azimuth_forward",
    )(block_order, arrived, cosine, sine, left, right)


def back_kernel(
    here_ref,
    before_ref,
    after_ref,
    halo_ref,
    coefficient_ref,
    offset_ref,
    spectra_ref,
    right_ref,
    left_ref,
    cosine_ref,
    sine_ref,
    out_ref,
    filtered,
    turned,
):
    tile = pl.program_id(0)
    step = pl.program_id(1)
    blocks, groups, rows, _ = here_ref.shape
    outer_size = rows // 2
    chunks = FACTOR // groups
    last = pl.num_programs(0) - 1

    @pl.when(step < chunks)
    def _():
        shape = (FACTOR + 2 * MARGIN_BINS, FACTOR)
        row = lax.broadcasted_iota(jnp.int32, shape, 0)
        lane = lax.broadcasted_iota(jnp.int32, shape, 1)
        kept = FACTOR + MARGIN_BINS
        spot = jnp.where(row < kept, row, row - shape[0])
        column = (spot + MARGIN_BINS - lane).astype(jnp.float32).astype(jnp.bfloat16)
        blank = jnp.zeros((FACTOR - 2 * MARGIN_BINS, FACTOR), jnp.bfloat16)
        side = lax.broadcasted_iota(jnp.int32, (rows, FACTOR), 1)

        def one_group(g, carry):
            gap = column - offset_ref[0, pl.ds(g, 1), :].astype(jnp.bfloat16)
            taps = coefficient_ref[0, g]
            table = jnp.zeros(shape, jnp.bfloat16)
            for s in range(KERNEL):
                table = jnp.where(
                    gap == jnp.bfloat16(s), taps[s : s + 1, :].astype(jnp.bfloat16), table
                )
            table = jnp.concatenate([table[:kept], blank, table[kept:]], axis=0)
            windows = []
            for b in range(blocks):
                halo = halo_ref[b, g].astype(jnp.float32)
                after = jnp.where(tile == last, halo, after_ref[b, g].astype(jnp.float32))
                before = jnp.where(tile == 0, halo, before_ref[b, g].astype(jnp.float32))
                edges = jnp.where(side < BAND_BINS, after, before).astype(jnp.bfloat16)
                windows.append(jnp.concatenate([here_ref[b, g], edges], axis=1))
            moved = jnp.dot(
                jnp.concatenate(windows, axis=0), table, preferred_element_type=jnp.float32
            )
            spec_real, spec_imag = spectra_ref[0, g, :outer_size], spectra_ref[0, g, outer_size:]
            start = pl.multiple_of((step * groups + g) * rows, rows)
            for b in range(blocks):
                re = moved[b * rows : b * rows + outer_size]
                im = moved[b * rows + outer_size : (b + 1) * rows]
                filtered[b, pl.ds(start, outer_size), :] = re * spec_real + im * spec_imag
                filtered[b, pl.ds(start + outer_size, outer_size), :] = (
                    im * spec_real - re * spec_imag
                )
            return carry

        lax.fori_loop(0, groups, one_group, 0, unroll=4)

    @pl.when(step >= chunks)
    def _():
        b = jnp.maximum(step - chunks, 0)
        right = right_ref[...]
        left = left_ref[...]

        def one_row(k, carry):
            signal = jnp.concatenate(
                [filtered[b, pl.ds(k + c * outer_size, FACTOR, stride=rows), :] for c in range(2)],
                axis=0,
            ).astype(jnp.bfloat16)
            returned = lax.dot_general(
                signal, right, (((0,), (0,)), ((), ())), preferred_element_type=jnp.float32
            )
            cosine, sine = cosine_ref[pl.ds(k, 1), :], sine_ref[pl.ds(k, 1), :]
            re, im = returned[:, :FACTOR], returned[:, FACTOR:]
            turned[pl.ds(k, FACTOR, stride=rows), :] = re * cosine - im * sine
            turned[pl.ds(k + outer_size, FACTOR, stride=rows), :] = re * sine + im * cosine
            return carry

        lax.fori_loop(0, outer_size, one_row, 0, unroll=4)
        wide = left.shape[0]
        each = wide // rows

        def some_bins(r, carry):
            start = pl.multiple_of(r * wide, wide)
            signal = turned[pl.ds(start, wide), :].astype(jnp.bfloat16)
            lines = jnp.dot(left, signal, preferred_element_type=jnp.float32) * (1.0 / PULSES)
            out_ref[0, pl.ds(r * each, each)] = lines.reshape(each, rows, FACTOR).astype(
                jnp.bfloat16
            )
            return carry

        lax.fori_loop(0, FACTOR // each, some_bins, 0, unroll=4)


def back_azimuth(spectral, halo, spectra, coefficients, offsets, tables):
    blocks, _, rows, width = spectral.shape
    tiles = width // FACTOR
    outer_size = rows // 2
    groups = 8
    chunks = FACTOR // groups
    per_tile = FACTOR // BAND_BINS
    taps = (
        coefficients.reshape(tiles, per_tile, KERNEL, BAND_BINS, FACTOR)
        .transpose(0, 4, 2, 1, 3)
        .reshape(tiles, FACTOR, KERNEL, FACTOR)
        .astype(jnp.float32)
    )
    shifts = jnp.repeat(
        offsets.reshape(tiles, per_tile, FACTOR).transpose(0, 2, 1), BAND_BINS, axis=2
    ).astype(jnp.float32)
    doppler = jnp.repeat(
        spectra.reshape(tiles, per_tile, outer_size, 2, FACTOR)
        .transpose(0, 4, 3, 2, 1)
        .reshape(tiles, FACTOR, rows, per_tile),
        BAND_BINS,
        axis=3,
    )
    right = tables[4].reshape(2 * FACTOR, 2 * FACTOR)
    small = tables[3].transpose(1, 0, 2, 3).reshape(rows, rows)
    left = jnp.kron(jnp.eye(2 * FACTOR // rows, dtype=jnp.float32), small.astype(jnp.float32))
    left = left.astype(jnp.bfloat16)

    def at(s):
        return jnp.minimum(s, chunks - 1)

    def piece(shift):
        return pl.BlockSpec(
            (blocks, groups, rows, FACTOR),
            lambda t, s: (0, at(s), 0, jnp.clip(t + shift, 0, tiles - 1)),
        )

    def whole(array):
        return pl.BlockSpec(array.shape, lambda t, s: (0,) * array.ndim)

    cosine, sine = jnp.cos(tables[2]), jnp.sin(tables[2])
    image = pl.pallas_call(
        back_kernel,
        grid=(tiles, chunks + blocks),
        in_specs=[
            piece(0),
            piece(-1),
            piece(1),
            pl.BlockSpec((blocks, groups, rows, FACTOR), lambda t, s: (0, at(s), 0, 0)),
            pl.BlockSpec((1, groups, KERNEL, FACTOR), lambda t, s: (t, at(s), 0, 0)),
            pl.BlockSpec((1, groups, FACTOR), lambda t, s: (t, at(s), 0)),
            pl.BlockSpec((1, groups, rows, FACTOR), lambda t, s: (t, at(s), 0, 0)),
            whole(right),
            whole(left),
            whole(cosine),
            whole(sine),
        ],
        out_specs=pl.BlockSpec(
            (1, FACTOR, rows, FACTOR), lambda t, s: (jnp.maximum(s - chunks, 0), t, 0, 0)
        ),
        out_shape=jax.ShapeDtypeStruct((blocks, width, rows, FACTOR), jnp.bfloat16),
        scratch_shapes=[
            pltpu.VMEM((blocks, FACTOR * rows, FACTOR), jnp.float32),
            pltpu.VMEM((FACTOR * rows, FACTOR), jnp.float32),
        ],
        compiler_params=pltpu.CompilerParams(vmem_limit_bytes=44 * 2**20),
        name="azimuth_back",
    )(
        spectral,
        spectral,
        spectral,
        halo,
        taps,
        shifts,
        doppler,
        right,
        left,
        cosine,
        sine,
    )
    return (
        image.reshape(blocks, width, outer_size, 2, FACTOR)
        .transpose(0, 1, 3, 2, 4)
        .reshape(blocks, width, 2, outer_size * FACTOR)
    )


def halo_of(spectral):
    axes = ("section", "band")
    count = lax.axis_size(axes)
    up = [(i, i + 1) for i in range(count - 1)]
    down = [(i + 1, i) for i in range(count - 1)]
    width = spectral.shape[3]
    before = lax.ppermute(spectral[..., width - MARGIN_BINS :], axes, up)
    after = lax.ppermute(spectral[..., :MARGIN_BINS], axes, down)
    middle = jnp.zeros(spectral.shape[:3] + (FACTOR - 2 * MARGIN_BINS,), spectral.dtype)
    return jnp.concatenate([after, middle, before], axis=3)


def on_device(echoes, replica, azimuth_taps, coefficients, offsets, block_order):
    sections = lax.axis_size("section")
    bands = lax.axis_size("band")
    count = sections * bands
    direct = (RANGE_BINS // FACTOR) == 4 * count and echoes.shape[1] % 16 == 0
    range_tables = make_tables(RANGE_BINS)
    pulse_tables = make_tables(PULSES)
    range_spectrum = exact_spectrum(replica[None], RANGE_BINS)[0]
    spectra = exact_spectrum(azimuth_taps, PULSES)
    if direct:
        arrived = compress_and_turn(
            echoes, range_spectrum, (("section", sections), ("band", bands))
        )
        spectral = forward_azimuth(arrived, block_order, pulse_tables)
        return back_azimuth(
            spectral, halo_of(spectral), spectra, coefficients, offsets, pulse_tables
        )
    band_spectra = jnp.repeat(jnp.transpose(spectra, (1, 2, 3, 0)), BAND_BINS, axis=3)
    migration_table = build_migration(coefficients, offsets)
    images = []
    for position in range(BLOCKS):
        signal = lax.dynamic_index_in_dim(echoes, block_order[position], 0, keepdims=False)
        compressed = compress_range(signal, range_spectrum, range_tables)
        turned = corner_turn(compressed[:, None])
        images.append(focus_azimuth(turned[:, 0], migration_table, band_spectra, pulse_tables))
    return jnp.stack(images, axis=0)


def solution(mesh):
    in_specs = (
        P(None, ("band", "section"), None, None),
        P(),
        P(("section", "band"), None, None),
        P(("section", "band"), None, None, None),
        P(("section", "band"), None),
        P(),
    )
    out_specs = P(None, ("section", "band"), None, None)
    return jax.shard_map(
        on_device, mesh=mesh, in_specs=in_specs, out_specs=out_specs, check_vma=False
    )
```

```python
import functools
import math

import jax
import jax.numpy as jnp
from jax import lax
from jax.experimental import pallas as pl
from jax.experimental.pallas import tpu as pltpu
from jax.sharding import PartitionSpec as P

RANGE_BINS = 16384
PULSES = 4096
FACTOR = 128
BAND_BINS = 64
MARGIN_BINS = 32
KERNEL = 8
BLOCKS = 2


def extended(cells, sides, width):
    for axis, dim in sides:
        count = lax.axis_size(axis)
        ends = count - 1
        head = lax.slice_in_dim(cells, 0, width, axis=dim)
        tail = lax.slice_in_dim(cells, cells.shape[dim] - width, cells.shape[dim], axis=dim)
        cells = jnp.concatenate(
            [
                lax.ppermute(tail, axis, [(i, (i + 1) % count) for i in range(ends)]),
                cells,
                lax.ppermute(head, axis, [((i + 1) % count, i) for i in range(ends)]),
            ],
            axis=dim,
        )
    return cells


def phases(outer_size, inner_size, length):
    outer_index = jnp.arange(outer_size, dtype=jnp.int32)[:, None]
    inner_index = jnp.arange(inner_size, dtype=jnp.int32)[None, :]
    return 2.0 * math.pi / length * (outer_index * inner_index % length).astype(jnp.float32)


def left_matrix(phase_table, signum):
    cosine = jnp.cos(phase_table)
    sine_part = signum * jnp.sin(phase_table)
    upper_rows = jnp.stack([cosine, -sine_part], axis=1)
    lower_rows = jnp.stack([sine_part, cosine], axis=1)
    return jnp.stack([upper_rows, lower_rows], axis=0)


def right_matrix(phase_table, signum):
    cosine = jnp.cos(phase_table)
    sine_part = signum * jnp.sin(phase_table)
    leading = jnp.stack([cosine, sine_part], axis=1)
    trailing = jnp.stack([-sine_part, cosine], axis=1)
    return jnp.stack([leading, trailing], axis=0)


def rotate_by(real_part, imag_part, phase_table, signum):
    cosine = jnp.cos(phase_table)
    sine_part = signum * jnp.sin(phase_table)
    return (real_part * cosine - imag_part * sine_part, real_part * sine_part + imag_part * cosine)


def make_tables(length):
    outer_size = length // FACTOR
    outer_phase = phases(outer_size, outer_size, outer_size)
    inner_phase = phases(FACTOR, FACTOR, FACTOR)
    twist_phase = phases(outer_size, FACTOR, length)
    return (
        left_matrix(outer_phase, -1.0).astype(jnp.bfloat16),
        right_matrix(inner_phase, -1.0).astype(jnp.bfloat16),
        twist_phase,
        left_matrix(outer_phase, 1.0).astype(jnp.bfloat16),
        right_matrix(inner_phase, 1.0).astype(jnp.bfloat16),
    )


def contract(pattern, left_side, right_side):
    return jnp.einsum(pattern, left_side, right_side, preferred_element_type=jnp.float32)


def exact_spectrum(tap_rows, length):
    outer_size = length // FACTOR
    padded = jnp.pad(tap_rows, ((0, 0), (0, 0), (0, length - tap_rows.shape[2])))
    padded = padded.reshape(tap_rows.shape[0], 2, outer_size, FACTOR)
    outer_phase = phases(outer_size, outer_size, outer_size)
    inner_phase = phases(FACTOR, FACTOR, FACTOR)
    twist_phase = phases(outer_size, FACTOR, length)
    mixed_rows = jnp.einsum(
        "ckdn,bdnm->bckm", left_matrix(outer_phase, -1.0), padded, precision=lax.Precision.HIGHEST
    )
    real_part, imag_part = rotate_by(mixed_rows[:, 0], mixed_rows[:, 1], twist_phase, -1.0)
    rotated = jnp.stack([real_part, imag_part], axis=1)
    return jnp.einsum(
        "bdkn,dnem->bkem", rotated, right_matrix(inner_phase, -1.0), precision=lax.Precision.HIGHEST
    )


def matched(values, spectrum):
    real_part = values[..., 0, :]
    imag_part = values[..., 1, :]
    spec_real = spectrum[..., 0, :]
    spec_imag = spectrum[..., 1, :]
    return jnp.stack(
        [
            real_part * spec_real + imag_part * spec_imag,
            imag_part * spec_real - real_part * spec_imag,
        ],
        axis=-2,
    ).astype(jnp.bfloat16)


def compress_range(signal, spectrum, tables):
    pulse_rows = signal.shape[0]
    outer_size = RANGE_BINS // FACTOR
    mixed_rows = contract(
        "ckdn,bdnm->bckm", tables[0], signal.reshape(pulse_rows, 2, outer_size, FACTOR)
    )
    real_part, imag_part = rotate_by(mixed_rows[:, 0], mixed_rows[:, 1], tables[2], -1.0)
    rotated = jnp.stack([real_part, imag_part], axis=1).astype(jnp.bfloat16)
    spectral = contract("bdkn,dnem->bkem", rotated, tables[1])
    filtered = matched(spectral, spectrum)
    returned = contract("bkdn,dnem->bkem", filtered, tables[4])
    real_part, imag_part = rotate_by(returned[:, :, 0], returned[:, :, 1], tables[2], 1.0)
    turned = jnp.stack([real_part, imag_part], axis=1).astype(jnp.bfloat16)
    lines = (contract("cmek,bekq->bcmq", tables[3], turned) * (1.0 / RANGE_BINS)).astype(
        jnp.bfloat16
    )
    return lines.reshape(pulse_rows, 2, RANGE_BINS)


def build_migration(coefficients, offsets):
    columns = jnp.arange(BAND_BINS + 2 * MARGIN_BINS, dtype=jnp.int32)[None, None, :, None]
    targets = (
        jnp.arange(BAND_BINS, dtype=jnp.int32)[None, :, None, None] + offsets[:, None, None, :]
    )
    migration_table = jnp.zeros(
        (coefficients.shape[0], BAND_BINS, BAND_BINS + 2 * MARGIN_BINS, coefficients.shape[3]),
        jnp.float32,
    )
    for tap_index in range(KERNEL):
        weights = coefficients[:, tap_index, :, None, :].astype(jnp.float32)
        migration_table = migration_table + jnp.where(
            columns == targets + tap_index, weights, jnp.zeros((), jnp.float32)
        )
    return migration_table.astype(jnp.bfloat16)


def migrate(padded, migration_table):
    range_rows = padded.shape[3] - 2 * MARGIN_BINS
    band_count = range_rows // BAND_BINS
    lead = padded.shape[:3]
    head_rows = padded[..., :range_rows].reshape(lead + (band_count, BAND_BINS))
    tail_rows = padded[..., BAND_BINS : BAND_BINS + range_rows].reshape(
        lead + (band_count, BAND_BINS)
    )
    window = jnp.concatenate([head_rows, tail_rows], axis=4)
    shifted = contract("jitg,kcgjt->kcgji", migration_table, window)
    return shifted.reshape(lead + (range_rows,))


def focus_azimuth(turned, migration_table, band_spectra, tables):
    range_rows = turned.shape[2]
    outer_size = PULSES // FACTOR
    signal = turned.reshape(outer_size, FACTOR, 2, range_rows)
    mixed_rows = contract("ckdn,nmdr->kmcr", tables[0], signal)
    twist = tables[2][:, :, None]
    real_part, imag_part = rotate_by(mixed_rows[:, :, 0], mixed_rows[:, :, 1], twist, -1.0)
    rotated = jnp.stack([real_part, imag_part], axis=2).astype(jnp.bfloat16)
    spectral = contract("kndr,dnem->kemr", rotated, tables[1]).astype(jnp.bfloat16)
    padded = extended(spectral, ((("section", "band"), 3),), MARGIN_BINS)
    moved = migrate(padded, migration_table)
    real_part = moved[:, 0]
    imag_part = moved[:, 1]
    spec_real = band_spectra[:, 0]
    spec_imag = band_spectra[:, 1]
    filtered = jnp.stack(
        [
            real_part * spec_real + imag_part * spec_imag,
            imag_part * spec_real - real_part * spec_imag,
        ],
        axis=1,
    ).astype(jnp.bfloat16)
    returned = contract("kdnr,dnem->kemr", filtered, tables[4])
    real_part, imag_part = rotate_by(returned[:, 0], returned[:, 1], twist, 1.0)
    back = jnp.stack([real_part, imag_part], axis=1).astype(jnp.bfloat16)
    focused = (contract("cmek,keqr->rcmq", tables[3], back) * (1.0 / PULSES)).astype(jnp.bfloat16)
    return focused.reshape(range_rows, 2, PULSES)


def corner_turn(compressed):
    pulse_rows = compressed.shape[0]
    block_count = compressed.shape[1]
    sections = lax.axis_size("section")
    band_count = lax.axis_size("band")
    local_rows = RANGE_BINS // (sections * band_count)
    shaped = compressed.reshape(1, 1, pulse_rows, block_count, 2, sections, band_count, local_rows)
    across_bands = lax.all_to_all(shaped, "band", split_axis=6, concat_axis=0, tiled=True)
    across_sections = lax.all_to_all(
        across_bands, "section", split_axis=5, concat_axis=1, tiled=True
    )
    arrived = across_sections.reshape(
        band_count * sections * pulse_rows, block_count, 2, local_rows
    )
    return arrived


def compress_send_kernel(
    axes,
    x_ref,
    left_ref,
    right_ref,
    right_back_ref,
    left_back_ref,
    cosine_ref,
    sine_ref,
    spec_real_ref,
    spec_imag_ref,
    arrived_ref,
    outbox,
    send_sem,
    recv_sem,
    local_sem,
):
    (major, major_size), (minor, minor_size) = axes
    count = major_size * minor_size
    step = pl.program_id(0)
    steps = pl.num_programs(0)
    pairs = outbox.shape[2]
    per_block = arrived_ref.shape[2] // pairs
    block = step // per_block
    first = (step % per_block) * pairs
    me = lax.axis_index(major) * minor_size + lax.axis_index(minor)
    source = lax.axis_index(minor) * major_size + lax.axis_index(major)

    @pl.when(step == 0)
    def _():
        barrier = pltpu.get_barrier_semaphore()

        def greet(k, carry):
            other = (me + k) % count
            pl.semaphore_signal(
                barrier,
                inc=1,
                device_id={major: other // minor_size, minor: other % minor_size},
                device_id_type=pl.DeviceIdType.MESH,
            )
            return carry

        lax.fori_loop(1, count, greet, 0)
        pl.semaphore_wait(barrier, count - 1)

    left = left_ref[...]
    right = right_ref[...]
    right_back = right_back_ref[...]
    left_back = left_back_ref[...]
    half = FACTOR

    def one_pair(pair, carry):
        cosine = cosine_ref[...]
        sine = sine_ref[...]
        spec_real = spec_real_ref[...]
        spec_imag = spec_imag_ref[...]
        signal = jnp.concatenate([x_ref[0, 2 * pair], x_ref[0, 2 * pair + 1]], axis=1)
        mixed = jnp.dot(left, signal, preferred_element_type=jnp.float32)
        rows = []
        for p in range(2):
            lanes = slice(p * half, (p + 1) * half)
            re, im = mixed[:half, lanes], mixed[half:, lanes]
            rows.append(
                jnp.concatenate([re * cosine + im * sine, im * cosine - re * sine], axis=1).astype(
                    jnp.bfloat16
                )
            )
        spectral = jnp.dot(
            jnp.concatenate(rows, axis=0), right, preferred_element_type=jnp.float32
        )
        rows = []
        for p in range(2):
            part = spectral[p * half : (p + 1) * half]
            re, im = part[:, :half], part[:, half:]
            rows.append(
                jnp.concatenate(
                    [re * spec_real + im * spec_imag, im * spec_real - re * spec_imag], axis=1
                ).astype(jnp.bfloat16)
            )
        returned = jnp.dot(
            jnp.concatenate(rows, axis=0), right_back, preferred_element_type=jnp.float32
        )
        columns = []
        for p in range(2):
            part = returned[p * half : (p + 1) * half]
            re, im = part[:, :half], part[:, half:]
            columns.append(
                jnp.concatenate([re * cosine - im * sine, re * sine + im * cosine], axis=0).astype(
                    jnp.bfloat16
                )
            )
        lines = jnp.dot(
            left_back, jnp.concatenate(columns, axis=1), preferred_element_type=jnp.float32
        ) * (1.0 / RANGE_BINS)
        tile = lines.shape[0] // count
        packed = jnp.concatenate(
            [
                lines[:, :half].reshape(count, tile, half),
                lines[:, half:].reshape(count, tile, half),
            ],
            axis=1,
        ).astype(jnp.bfloat16)
        outbox[step, :, pair] = packed
        return carry

    lax.fori_loop(0, pairs, one_pair, 0)

    own = pltpu.make_async_copy(
        outbox.at[step, me], arrived_ref.at[block, source, pl.ds(first, pairs)], local_sem
    )
    own.start()

    def post(k, carry):
        other = (me + k * 11) % count
        pltpu.make_async_remote_copy(
            src_ref=outbox.at[step, other],
            dst_ref=arrived_ref.at[block, source, pl.ds(first, pairs)],
            send_sem=send_sem,
            recv_sem=recv_sem,
            device_id={major: other // minor_size, minor: other % minor_size},
            device_id_type=pl.DeviceIdType.MESH,
        ).start()
        return carry

    lax.fori_loop(1, count, post, 0)
    own.wait()

    @pl.when(step == steps - 1)
    def _():
        whole = arrived_ref.at[:, pl.ds(0, count - 1)]
        pltpu.make_async_copy(whole, whole, send_sem).wait()
        pltpu.make_async_copy(whole, whole, recv_sem).wait()


def compress_and_turn(echoes, spectrum, axes):
    blocks, pulses, _, length = echoes.shape
    count = axes[0][1] * axes[1][1]
    outer_size = length // FACTOR
    rows_each = outer_size // count
    chunk = 16
    signal = (
        echoes.reshape(blocks, pulses, 2, outer_size, FACTOR)
        .transpose(0, 1, 3, 2, 4)
        .reshape(blocks, pulses, 2 * outer_size, FACTOR)
    )
    tables = make_tables(length)
    left = tables[0].transpose(0, 1, 3, 2).reshape(2 * outer_size, 2 * outer_size)
    right = tables[1].reshape(2 * FACTOR, 2 * FACTOR)
    right_back = tables[4].reshape(2 * FACTOR, 2 * FACTOR)
    left_back = (
        tables[3]
        .reshape(2, count, rows_each, 2 * outer_size)
        .transpose(1, 0, 2, 3)
        .reshape(2 * outer_size, 2 * outer_size)
    )
    steps_per_block = pulses // chunk
    steps = blocks * steps_per_block
    pairs = chunk // 2
    tile = 4 * rows_each

    def whole(array):
        return pl.BlockSpec(array.shape, lambda s: (0,) * array.ndim)

    operands = (
        left,
        right,
        right_back,
        left_back,
        jnp.cos(tables[2]),
        jnp.sin(tables[2]),
        spectrum[:, 0],
        spectrum[:, 1],
    )
    return pl.pallas_call(
        functools.partial(compress_send_kernel, axes),
        grid=(steps,),
        in_specs=[
            pl.BlockSpec(
                (1, chunk, 2 * outer_size, FACTOR),
                lambda s: (s // steps_per_block, s % steps_per_block, 0, 0),
            )
        ]
        + [whole(array) for array in operands],
        out_specs=pl.BlockSpec(memory_space=pl.ANY),
        out_shape=jax.ShapeDtypeStruct(
            (blocks, count, pulses // 2, tile, FACTOR), jnp.bfloat16
        ),
        scratch_shapes=[
            pltpu.VMEM((steps, count, pairs, tile, FACTOR), jnp.bfloat16),
            pltpu.SemaphoreType.DMA,
            pltpu.SemaphoreType.DMA,
            pltpu.SemaphoreType.DMA,
        ],
        compiler_params=pltpu.CompilerParams(
            collective_id=0, has_side_effects=True, vmem_limit_bytes=44 * 2**20
        ),
        cost_estimate=pl.CostEstimate(
            flops=blocks * pulses * 16 * FACTOR**2 * 2 * FACTOR,
            bytes_accessed=4 * echoes.size,
            transcendentals=0,
        ),
        name="compress_turn",
    )(signal, *operands)


def forward_kernel(
    order_ref, x_ref, cosine_ref, sine_ref, left_ref, right_ref, out_ref, lifted, mixed, spread
):
    step = pl.program_id(1)
    chunk = x_ref.shape[2]
    outer_size = x_ref.shape[1]
    tile = x_ref.shape[3]
    tiles = mixed.shape[0]
    rows = 2 * outer_size
    chunks = FACTOR // (2 * chunk)

    @pl.when(step < chunks)
    def _():
        lifted[...] = x_ref[0].reshape(outer_size * chunk * tile, FACTOR).astype(jnp.float32)
        left = left_ref[...]

        def one_column(n, carry):
            base = n * (tile // 2)
            parts = []
            for j in range(tiles):
                parts.append(
                    jnp.concatenate(
                        [
                            lifted[pl.ds(base + c * tiles + j, outer_size, stride=chunk * tile), :]
                            for c in range(2)
                        ],
                        axis=0,
                    )
                )
            signal = jnp.concatenate(parts, axis=1).astype(jnp.bfloat16)
            product = jnp.dot(left, signal, preferred_element_type=jnp.float32)
            cosine, sine = cosine_ref[n], sine_ref[n]
            start = pl.multiple_of((step * 2 * chunk + n) * rows, rows)
            for j in range(tiles):
                lanes = slice(j * FACTOR, (j + 1) * FACTOR)
                re, im = product[:outer_size, lanes], product[outer_size:, lanes]
                mixed[j, pl.ds(start, outer_size), :] = re * cosine + im * sine
                mixed[j, pl.ds(start + outer_size, outer_size), :] = im * cosine - re * sine
            return carry

        lax.fori_loop(0, 2 * chunk, one_column, 0, unroll=8)

    @pl.when(step >= chunks)
    def _():
        right = right_ref[...]
        j = jnp.maximum(step - chunks, 0)

        def one_row(k, carry):
            signal = jnp.concatenate(
                [mixed[j, pl.ds(k + c * outer_size, FACTOR, stride=rows), :] for c in range(2)],
                axis=0,
            ).astype(jnp.bfloat16)
            product = jnp.dot(right, signal, preferred_element_type=jnp.float32)
            for c in range(2):
                spread[pl.ds(k + c * outer_size, FACTOR, stride=rows), :] = product[
                    c * FACTOR : (c + 1) * FACTOR
                ]
            return carry

        lax.fori_loop(0, outer_size, one_row, 0, unroll=8)
        out_ref[0] = spread[...].reshape(FACTOR, rows, FACTOR).astype(jnp.bfloat16)


def forward_azimuth(arrived, block_order, tables):
    blocks, outer_size, pairs, tile, _ = arrived.shape
    tiles = tile // 4
    rows = 2 * outer_size
    chunk = 8
    chunks = pairs // chunk
    left = tables[0].reshape(rows, rows)
    right = tables[1].reshape(2 * FACTOR, 2 * FACTOR).T
    cosine = jnp.broadcast_to(jnp.cos(tables[2]).T[:, :, None], (FACTOR, outer_size, FACTOR))
    sine = jnp.broadcast_to(jnp.sin(tables[2]).T[:, :, None], (FACTOR, outer_size, FACTOR))
    twist = pl.BlockSpec(
        (2 * chunk, outer_size, FACTOR), lambda b, s, order: (jnp.minimum(s, chunks - 1), 0, 0)
    )
    return pl.pallas_call(
        forward_kernel,
        grid_spec=pltpu.PrefetchScalarGridSpec(
            num_scalar_prefetch=1,
            grid=(blocks, chunks + tiles),
            in_specs=[
                pl.BlockSpec(
                    (1, outer_size, chunk, tile, FACTOR),
                    lambda b, s, order: (order[b], 0, jnp.minimum(s, chunks - 1), 0, 0),
                ),
                twist,
                twist,
                pl.BlockSpec(left.shape, lambda b, s, order: (0, 0)),
                pl.BlockSpec(right.shape, lambda b, s, order: (0, 0)),
            ],
            out_specs=pl.BlockSpec(
                (1, FACTOR, rows, FACTOR),
                lambda b, s, order: (b, 0, 0, jnp.maximum(s - chunks, 0)),
            ),
            scratch_shapes=[
                pltpu.VMEM((outer_size * chunk * tile, FACTOR), jnp.float32),
                pltpu.VMEM((tiles, FACTOR * rows, FACTOR), jnp.float32),
                pltpu.VMEM((FACTOR * rows, FACTOR), jnp.float32),
            ],
        ),
        out_shape=jax.ShapeDtypeStruct((blocks, FACTOR, rows, tiles * FACTOR), jnp.bfloat16),
        compiler_params=pltpu.CompilerParams(vmem_limit_bytes=44 * 2**20),
        name="azimuth_forward",
    )(block_order, arrived, cosine, sine, left, right)


def back_kernel(
    here_ref,
    before_ref,
    after_ref,
    halo_ref,
    coefficient_ref,
    offset_ref,
    spectra_ref,
    right_ref,
    left_ref,
    cosine_ref,
    sine_ref,
    out_ref,
    filtered,
    turned,
):
    tile = pl.program_id(0)
    step = pl.program_id(1)
    blocks, groups, rows, _ = here_ref.shape
    outer_size = rows // 2
    chunks = FACTOR // groups
    last = pl.num_programs(0) - 1

    @pl.when(step < chunks)
    def _():
        shape = (FACTOR + 2 * MARGIN_BINS, FACTOR)
        row = lax.broadcasted_iota(jnp.int32, shape, 0)
        lane = lax.broadcasted_iota(jnp.int32, shape, 1)
        kept = FACTOR + MARGIN_BINS
        spot = jnp.where(row < kept, row, row - shape[0])
        column = (spot + MARGIN_BINS - lane).astype(jnp.float32).astype(jnp.bfloat16)
        blank = jnp.zeros((FACTOR - 2 * MARGIN_BINS, FACTOR), jnp.bfloat16)
        side = lax.broadcasted_iota(jnp.int32, (rows, FACTOR), 1)

        def one_group(g, carry):
            gap = column - offset_ref[0, pl.ds(g, 1), :].astype(jnp.bfloat16)
            taps = coefficient_ref[0, g]
            table = jnp.zeros(shape, jnp.bfloat16)
            for s in range(KERNEL):
                table = jnp.where(
                    gap == jnp.bfloat16(s), taps[s : s + 1, :].astype(jnp.bfloat16), table
                )
            table = jnp.concatenate([table[:kept], blank, table[kept:]], axis=0)
            windows = []
            for b in range(blocks):
                halo = halo_ref[b, g].astype(jnp.float32)
                after = jnp.where(tile == last, halo, after_ref[b, g].astype(jnp.float32))
                before = jnp.where(tile == 0, halo, before_ref[b, g].astype(jnp.float32))
                edges = jnp.where(side < BAND_BINS, after, before).astype(jnp.bfloat16)
                windows.append(jnp.concatenate([here_ref[b, g], edges], axis=1))
            moved = jnp.dot(
                jnp.concatenate(windows, axis=0), table, preferred_element_type=jnp.float32
            )
            spec_real, spec_imag = spectra_ref[0, g, :outer_size], spectra_ref[0, g, outer_size:]
            start = pl.multiple_of((step * groups + g) * rows, rows)
            for b in range(blocks):
                re = moved[b * rows : b * rows + outer_size]
                im = moved[b * rows + outer_size : (b + 1) * rows]
                filtered[b, pl.ds(start, outer_size), :] = re * spec_real + im * spec_imag
                filtered[b, pl.ds(start + outer_size, outer_size), :] = (
                    im * spec_real - re * spec_imag
                )
            return carry

        lax.fori_loop(0, groups, one_group, 0, unroll=8)

    @pl.when(step >= chunks)
    def _():
        b = jnp.maximum(step - chunks, 0)
        right = right_ref[...]
        left = left_ref[...]

        def one_row(k, carry):
            signal = jnp.concatenate(
                [filtered[b, pl.ds(k + c * outer_size, FACTOR, stride=rows), :] for c in range(2)],
                axis=0,
            ).astype(jnp.bfloat16)
            returned = lax.dot_general(
                signal, right, (((0,), (0,)), ((), ())), preferred_element_type=jnp.float32
            )
            cosine, sine = cosine_ref[pl.ds(k, 1), :], sine_ref[pl.ds(k, 1), :]
            re, im = returned[:, :FACTOR], returned[:, FACTOR:]
            turned[pl.ds(k, FACTOR, stride=rows), :] = re * cosine - im * sine
            turned[pl.ds(k + outer_size, FACTOR, stride=rows), :] = re * sine + im * cosine
            return carry

        lax.fori_loop(0, outer_size, one_row, 0, unroll=8)
        wide = left.shape[0]
        each = wide // rows

        def some_bins(r, carry):
            start = pl.multiple_of(r * wide, wide)
            signal = turned[pl.ds(start, wide), :].astype(jnp.bfloat16)
            lines = jnp.dot(left, signal, preferred_element_type=jnp.float32) * (1.0 / PULSES)
            out_ref[0, pl.ds(r * each, each)] = lines.reshape(each, rows, FACTOR).astype(
                jnp.bfloat16
            )
            return carry

        lax.fori_loop(0, FACTOR // each, some_bins, 0, unroll=8)


def back_azimuth(spectral, halo, spectra, coefficients, offsets, tables):
    blocks, _, rows, width = spectral.shape
    tiles = width // FACTOR
    outer_size = rows // 2
    groups = 8
    chunks = FACTOR // groups
    per_tile = FACTOR // BAND_BINS
    taps = (
        coefficients.reshape(tiles, per_tile, KERNEL, BAND_BINS, FACTOR)
        .transpose(0, 4, 2, 1, 3)
        .reshape(tiles, FACTOR, KERNEL, FACTOR)
        .astype(jnp.float32)
    )
    shifts = jnp.repeat(
        offsets.reshape(tiles, per_tile, FACTOR).transpose(0, 2, 1), BAND_BINS, axis=2
    ).astype(jnp.float32)
    compact = (
        spectra.reshape(tiles, per_tile, outer_size, 2, FACTOR)
        .transpose(1, 0, 4, 3, 2)
        .reshape(per_tile, tiles, FACTOR, rows, 1)
    )
    lane = lax.broadcasted_iota(jnp.int32, (tiles, FACTOR, rows, FACTOR), 3)
    doppler = jnp.where(lane < BAND_BINS, compact[0], compact[1])
    right = tables[4].reshape(2 * FACTOR, 2 * FACTOR)
    small = tables[3].transpose(1, 0, 2, 3).reshape(rows, rows)
    left = jnp.kron(jnp.eye(2 * FACTOR // rows, dtype=jnp.float32), small.astype(jnp.float32))
    left = left.astype(jnp.bfloat16)

    def at(s):
        return jnp.minimum(s, chunks - 1)

    def piece(shift):
        return pl.BlockSpec(
            (blocks, groups, rows, FACTOR),
            lambda t, s: (0, at(s), 0, jnp.clip(t + shift, 0, tiles - 1)),
        )

    def whole(array):
        return pl.BlockSpec(array.shape, lambda t, s: (0,) * array.ndim)

    cosine, sine = jnp.cos(tables[2]), jnp.sin(tables[2])
    image = pl.pallas_call(
        back_kernel,
        grid=(tiles, chunks + blocks),
        in_specs=[
            piece(0),
            piece(-1),
            piece(1),
            pl.BlockSpec((blocks, groups, rows, FACTOR), lambda t, s: (0, at(s), 0, 0)),
            pl.BlockSpec((1, groups, KERNEL, FACTOR), lambda t, s: (t, at(s), 0, 0)),
            pl.BlockSpec((1, groups, FACTOR), lambda t, s: (t, at(s), 0)),
            pl.BlockSpec((1, groups, rows, FACTOR), lambda t, s: (t, at(s), 0, 0)),
            whole(right),
            whole(left),
            whole(cosine),
            whole(sine),
        ],
        out_specs=pl.BlockSpec(
            (1, FACTOR, rows, FACTOR), lambda t, s: (jnp.maximum(s - chunks, 0), t, 0, 0)
        ),
        out_shape=jax.ShapeDtypeStruct((blocks, width, rows, FACTOR), jnp.bfloat16),
        scratch_shapes=[
            pltpu.VMEM((blocks, FACTOR * rows, FACTOR), jnp.float32),
            pltpu.VMEM((FACTOR * rows, FACTOR), jnp.float32),
        ],
        compiler_params=pltpu.CompilerParams(vmem_limit_bytes=44 * 2**20),
        name="azimuth_back",
    )(
        spectral,
        spectral,
        spectral,
        halo,
        taps,
        shifts,
        doppler,
        right,
        left,
        cosine,
        sine,
    )
    return (
        image.reshape(blocks, width, outer_size, 2, FACTOR)
        .transpose(0, 1, 3, 2, 4)
        .reshape(blocks, width, 2, outer_size * FACTOR)
    )


def halo_of(spectral):
    axes = ("section", "band")
    count = lax.axis_size(axes)
    up = [(i, i + 1) for i in range(count - 1)]
    down = [(i + 1, i) for i in range(count - 1)]
    width = spectral.shape[3]
    before = lax.ppermute(spectral[..., width - MARGIN_BINS :], axes, up)
    after = lax.ppermute(spectral[..., :MARGIN_BINS], axes, down)
    middle = jnp.zeros(spectral.shape[:3] + (FACTOR - 2 * MARGIN_BINS,), spectral.dtype)
    return jnp.concatenate([after, middle, before], axis=3)


def on_device(echoes, replica, azimuth_taps, coefficients, offsets, block_order):
    sections = lax.axis_size("section")
    bands = lax.axis_size("band")
    count = sections * bands
    direct = (RANGE_BINS // FACTOR) == 4 * count and echoes.shape[1] % 16 == 0
    range_tables = make_tables(RANGE_BINS)
    pulse_tables = make_tables(PULSES)
    range_spectrum = exact_spectrum(replica[None], RANGE_BINS)[0]
    spectra = exact_spectrum(azimuth_taps, PULSES)
    if direct:
        arrived = compress_and_turn(
            echoes, range_spectrum, (("section", sections), ("band", bands))
        )
        spectral = forward_azimuth(arrived, block_order, pulse_tables)
        return back_azimuth(
            spectral, halo_of(spectral), spectra, coefficients, offsets, pulse_tables
        )
    band_spectra = jnp.repeat(jnp.transpose(spectra, (1, 2, 3, 0)), BAND_BINS, axis=3)
    migration_table = build_migration(coefficients, offsets)
    images = []
    for position in range(BLOCKS):
        signal = lax.dynamic_index_in_dim(echoes, block_order[position], 0, keepdims=False)
        compressed = compress_range(signal, range_spectrum, range_tables)
        turned = corner_turn(compressed[:, None])
        images.append(focus_azimuth(turned[:, 0], migration_table, band_spectra, pulse_tables))
    return jnp.stack(images, axis=0)


def solution(mesh):
    in_specs = (
        P(None, ("band", "section"), None, None),
        P(),
        P(("section", "band"), None, None),
        P(("section", "band"), None, None, None),
        P(("section", "band"), None),
        P(),
    )
    out_specs = P(None, ("section", "band"), None, None)
    return jax.shard_map(
        on_device, mesh=mesh, in_specs=in_specs, out_specs=out_specs, check_vma=False
    )
```
